32 devices in a mesh: shard: 4 (over y, x), ctx: 2 (over z_hi), tp: 4 (over z_lo, core).
Axes of the slice: x: 2, y: 2, z: 4 (z_hi: 2, z_lo: 2; z = z_hi * 2 + z_lo), core: 2. Of those that a mesh axis runs over, the one named last changes fastest.
Arguments:
- tokens_in: bfloat16 [2, 4, 384, 2048], P(None, 'shard', 'ctx'), may hold values from -6 to 6
- cotangent: bfloat16 [2, 4, 384, 2048], P(None, 'shard', 'ctx'), may hold values from -6 to 6
- expert_ids: int32 [2, 4, 384, 4], P(None, 'shard', 'ctx'), may hold values from 0 to 7, all different within a row; in each aligned block of 192 rows (0 to 191, 192 to 383, ..., all dimensions but the last counted through in order) at most 128 rows name the same one
- prefix_len: int32 [2, 4], P(None, 'shard'), may hold values from 0 to 384
- attn_gain: bfloat16 [2048], P('shard'), may hold values from 0.5 to 1.5
- qkv_weight: bfloat16 [3, 2048, 2048], P(None, 'shard', 'tp'), may hold values from -0.125 to 0.125
- qkv_bias: bfloat16 [3, 16, 128], P(None, 'tp'), may hold values from -1 to 1
- out_weight: bfloat16 [2048, 2048], P('tp', 'shard'), may hold values from -2 to 2
- ffn_gain: bfloat16 [2048], P('shard'), may hold values from 0.5 to 1.5
- router_weight: bfloat16 [2048, 8], P('shard'), may hold values from -0.0625 to 0.0625
- expert_gate: bfloat16 [8, 2048, 1408], P(None, 'shard', 'tp'), may hold values from -0.125 to 0.125
- expert_up: bfloat16 [8, 2048, 1408], P(None, 'shard', 'tp'), may hold values from -0.125 to 0.125
- expert_down: bfloat16 [8, 1408, 2048], P(None, 'tp', 'shard'), may hold values from -0.625 to 0.625
- shared_gate: bfloat16 [2048, 5632], P('shard', 'tp'), may hold values from -0.125 to 0.125
- shared_up: bfloat16 [2048, 5632], P('shard', 'tp'), may hold values from -0.125 to 0.125
- shared_down: bfloat16 [5632, 2048], P('tp', 'shard'), may hold values from -0.15625 to 0.15625
- shared_switch: bfloat16 [2048], P('shard'), may hold values from -0.125 to 0.125
Outputs:
- layer_out: bfloat16 [2, 4, 384, 2048], P(None, 'shard', 'ctx')
- tokens_grad: float32 [2, 4, 384, 2048], P(None, 'shard', 'ctx')
- attn_gain_grad: float32 [2048], P(('shard', 'ctx'))
- qkv_weight_grad: float32 [3, 2048, 2048], P(None, ('shard', 'ctx'), 'tp')
- qkv_bias_grad: float32 [3, 16, 128], P(None, 'tp', ('shard', 'ctx'))
- out_weight_grad: float32 [2048, 2048], P('tp', ('shard', 'ctx'))
- ffn_gain_grad: float32 [2048], P(('shard', 'ctx'))
- router_grad: float32 [2048, 8], P(('shard', 'ctx'))
- expert_gate_grad: float32 [8, 2048, 1408], P(None, ('shard', 'ctx'), 'tp')
- expert_up_grad: float32 [8, 2048, 1408], P(None, ('shard', 'ctx'), 'tp')
- expert_down_grad: float32 [8, 1408, 2048], P(None, 'tp', ('shard', 'ctx'))
- shared_gate_grad: float32 [2048, 5632], P(('shard', 'ctx'), 'tp')
- shared_up_grad: float32 [2048, 5632], P(('shard', 'ctx'), 'tp')
- shared_down_grad: float32 [5632, 2048], P('tp', ('shard', 'ctx'))
- switch_grad: float32 [2048], P(('shard', 'ctx'))
The draws below stay inside these ranges and needn't reach their ends.
Inputs may be any that keep to these rules, and one draw needn't show every extreme that they name: `expert_ids`: each token names 4 different experts. Among the 192 positions of a sequence that one index of ctx holds, no expert is named by more than 128 tokens, and one expert by exactly 128.
All inputs are finite; a program needn't handle non-finite values.
Results may differ from the reference program's by a relative error of at most 0.04.
Values may be sent and summed in bfloat16 or wider, within the bound.
No kernel may reach another device: no remote copies, remote signals or barrier semaphores. Data moves between devices by JAX's collectives and lax.ppermute only.
A program may use at most 320 MiB of HBM per device.

```python
import math
import jax
import jax.numpy as jnp
import numpy as np
from jax import lax

D = 2048
HEADS = 16
HEAD_DIM = 128
FF = 1408
SFF = 5632
TOPK = 4
EXPERTS = 8
MICRO = 2
SEQ = 384
BATCH = 4
TOK_DEV = 192
CAP = 128
N_CTX = 2


def touch_ends(array, rng, low, top_value):
    longest = array.shape.index(max(array.shape))
    spots = []
    for shift in (0, 1):
        where = [jax.random.randint(jax.random.fold_in(rng, axis), (), 0, length) for axis, length in enumerate(array.shape)]
        where[longest] = (where[longest] + shift) % array.shape[longest]
        spots.append(tuple(where))
    return array.at[spots[0]].set(low).at[spots[1]].set(top_value)


def level_of(rng, extent, split, smallest, largest):
    def one(axis_at, blocks):
        steps = jax.random.uniform(jax.random.fold_in(jax.random.fold_in(rng, 6), axis_at), (blocks,), jnp.float32, smallest / len(split), largest / len(split))
        return jnp.repeat(jnp.exp(steps), extent[axis_at] // blocks).reshape((-1,) + (1,) * (len(extent) - axis_at - 1))

    factor_of = one(*split[0])
    for cut in split[1:]:
        factor_of = factor_of * one(*cut)
    return factor_of


def deal_out(rng, own, number, rows, amount, top, bound, slope):
    ranking = jax.random.permutation(rng, amount)
    heavy_load, ordinary = load_shares(amount, rows * top, bound, slope, True), load_shares(amount, rows * top, bound, slope, False)
    places = jnp.arange(amount)

    def named(tallies, rotation):
        used = int((tallies > 0).sum())
        fixed = max(1, used // 4)
        moved = fixed + (places - fixed + rotation * (used - fixed)) % max(1, amount - fixed)
        return jnp.zeros((amount,), jnp.int32).at[ranking[jnp.where(places < fixed, places, moved)]].set(jnp.asarray(tallies, jnp.int32))

    tallies = jnp.where(number % 4 == 0, named(heavy_load, number // 4), named(ordinary, number - number // 4 - 1))
    mixed = jax.random.permutation(jax.random.fold_in(own, 3), amount)
    giver, taker = mixed[0:amount // 2 * 2:2], mixed[1:amount // 2 * 2:2]
    margin = jnp.minimum(tallies[giver] - 1, bound - tallies[taker]) // 2
    margin = jnp.where((giver == ranking[0]) | (taker == ranking[0]) | (tallies[taker] == 0), 0, jnp.maximum(margin, 0))
    moved = jax.random.randint(jax.random.fold_in(own, 4), (amount // 2,), 0, 1 << 20) % (margin + 1)
    tallies = tallies.at[giver].add(-moved).at[taker].add(moved)
    items = jnp.searchsorted(jnp.cumsum(tallies), jnp.arange(rows * top), side="right").astype(jnp.int32)
    listing = items.reshape(top, rows).T
    listing = listing[jax.random.permutation(jax.random.fold_in(own, 1), rows)]
    rotation = jax.random.randint(jax.random.fold_in(own, 2), (rows, 1), 0, top)
    return jnp.take_along_axis(listing, (jnp.arange(top)[None, :] + rotation) % top, axis=1)


def load_shares(count, total, bound, skew, full):
    loads = [(1 << 20) // math.isqrt(standing ** skew) + 1 for standing in range(1, count + 1)]
    largest = bound if full else min(bound, max(-(-total // count), total * loads[0] // sum(loads)))
    least = 1 if total - largest >= count - 1 else 0
    given, rest = [largest] + [least] * (count - 1), total - largest - least * (count - 1)
    while rest > 0:
        free = [i for i in range(1, count) if given[i] < largest] or [i for i in range(1, count) if given[i] < bound]
        pool, remaining = sum([loads[i] for i in free]), rest
        for i in free:
            more = min(bound - given[i], max(1, remaining * loads[i] // pool), rest)
            given[i] = given[i] + more
            rest = rest - more
    return np.array(given)


def bell_draw(key, shape, deviation, bound, pieces=(), kind=jnp.bfloat16):
    result = jax.random.normal(key, shape, jnp.float32) * deviation
    if len(pieces) > 0:
        result = level_of(key, shape, pieces, -0.22, 0.18) * result
    return jnp.clip(result, min=-bound, max=bound).astype(kind)


def setup_inputs(seed: int = 0) -> dict:
    key_list = jax.random.split(jax.random.key(seed), 18)
    tokens_in = bell_draw(key_list[0], (MICRO, BATCH, SEQ, D), 1.0, 6.0, ((1, 4), (2, 2)))
    cotangent = bell_draw(key_list[1], (MICRO, BATCH, SEQ, D), 1.0, 6.0, ((1, 4), (2, 2)))
    expert_ids_keys = jax.random.split(jax.random.fold_in(key_list[2], 1), MICRO * BATCH * SEQ // TOK_DEV)
    expert_ids_turns = jax.random.permutation(jax.random.fold_in(key_list[2], 3), MICRO * BATCH * SEQ // TOK_DEV)
    expert_ids = jax.vmap(lambda own, number: deal_out(jax.random.fold_in(key_list[2], 2), own, number, TOK_DEV, EXPERTS, TOPK, CAP, 1))(expert_ids_keys, expert_ids_turns).reshape((MICRO, BATCH, SEQ, TOPK))
    prefix_len = touch_ends(jax.random.randint(key_list[3], (MICRO, BATCH), 0, SEQ + 1), jax.random.fold_in(key_list[3], 1), 0, SEQ).astype(jnp.int32)
    attn_gain = jnp.clip(1.0 + 0.1 * jax.random.normal(key_list[4], (D,), jnp.float32), 0.5, 1.5).astype(jnp.bfloat16)
    qkv_weight = bell_draw(key_list[5], (3, D, HEADS * HEAD_DIM), D ** -0.5, 0.125, ((1, 4), (2, 4)))
    qkv_bias = bell_draw(key_list[6], (3, HEADS, HEAD_DIM), 0.2, 1.0, ((1, 4),))
    out_weight = bell_draw(key_list[7], (HEADS * HEAD_DIM, D), (HEADS * HEAD_DIM // 256) ** -0.5, 2.0, ((0, 4), (1, 4)))
    ffn_gain = jnp.clip(1.0 + 0.1 * jax.random.normal(key_list[8], (D,), jnp.float32), 0.5, 1.5).astype(jnp.bfloat16)
    router_weight = bell_draw(key_list[9], (D, EXPERTS), (4 * D) ** -0.5, 0.0625, ((0, 4),))
    expert_gate = bell_draw(key_list[10], (EXPERTS, D, FF), D ** -0.5, 0.125, ((1, 4), (2, 4)))
    expert_up = bell_draw(key_list[11], (EXPERTS, D, FF), D ** -0.5, 0.125, ((1, 4), (2, 4)))
    expert_down = bell_draw(key_list[12], (EXPERTS, FF, D), (FF // 16) ** -0.5, 0.625, ((1, 4), (2, 4)))
    shared_gate = bell_draw(key_list[13], (D, SFF), D ** -0.5, 0.125, ((0, 4), (1, 4)))
    shared_up = bell_draw(key_list[14], (D, SFF), D ** -0.5, 0.125, ((0, 4), (1, 4)))
    shared_down = bell_draw(key_list[15], (SFF, D), (SFF // 4) ** -0.5, 0.15625, ((0, 4), (1, 4)))
    shared_switch = bell_draw(key_list[16], (D,), D ** -0.5, 0.125, ((0, 4),))
    return dict(tokens_in=tokens_in, cotangent=cotangent, expert_ids=expert_ids, prefix_len=prefix_len, attn_gain=attn_gain, qkv_weight=qkv_weight, qkv_bias=qkv_bias, out_weight=out_weight, ffn_gain=ffn_gain, router_weight=router_weight, expert_gate=expert_gate, expert_up=expert_up, expert_down=expert_down, shared_gate=shared_gate, shared_up=shared_up, shared_down=shared_down, shared_switch=shared_switch)


@jax.custom_vjp
def low(v):
    return lax.optimization_barrier(v.astype(jnp.bfloat16)).astype(jnp.float32)

@jax.custom_vjp
def low_back(v):
    return v

def low_keep(v):
    return (low(v), None)

def low_pass(kept, grad):
    return (grad,)

def back_keep(v):
    return (v, None)

def back_low(kept, grad):
    return (low(grad),)
low.defvjp(low_keep, low_pass)
low_back.defvjp(back_keep, back_low)
epsilon = 1e-06
rope_base = 1000000.0
highest = lax.Precision.HIGHEST

def rms_scale(values, gain_vec):
    factor = lax.rsqrt(lax.optimization_barrier(jnp.mean(values * values, axis=-1, keepdims=True)) + epsilon)
    return values * factor * gain_vec

def rope_tables(length, head_dim):
    half_dim = head_dim // 2
    frequency = rope_base ** (-(jnp.arange(half_dim, dtype=jnp.float32) * 2.0) / head_dim)
    places = jnp.arange(length, dtype=jnp.float32)[:, None] * frequency[None, :]
    return (jnp.cos(places)[:, None, :], jnp.sin(places)[:, None, :])

def rotate(values, cosine, sine_table):
    half_dim = values.shape[-1] // 2
    first_half = values[..., :half_dim]
    second_half = values[..., half_dim:]
    return jnp.concatenate([first_half * cosine - second_half * sine_table, second_half * cosine + first_half * sine_table], axis=-1)

def dispatch(id_rows, experts, slot_room):
    token_count = id_rows.shape[0]
    pick_count = id_rows.shape[1]
    flat_ids = id_rows.reshape(-1).astype(jnp.int32)
    expert_marks = (flat_ids[:, None] == jnp.arange(experts, dtype=jnp.int32)[None, :]).astype(jnp.int32)
    expert_rank = lax.optimization_barrier(jnp.sum((jnp.cumsum(expert_marks, axis=0).astype(jnp.int32) - 1) * expert_marks, axis=1)).astype(jnp.int32)
    slot_index = (flat_ids * slot_room + expert_rank).astype(jnp.int32)
    token_owner = (jnp.arange(token_count * pick_count, dtype=jnp.int32) // pick_count).astype(jnp.int32)
    slot_owner = jnp.full((experts * slot_room,), token_count, jnp.int32).at[slot_index].set(token_owner)
    return (slot_index, slot_owner)

def sequence_forward(params, tokens_seq, ids_seq, prefix_value):
    attn_gain, qkv_weight, qkv_bias, out_weight, ffn_gain, router_weight, expert_gate, expert_up, expert_down, shared_gate, shared_up, shared_down, shared_switch = params
    normed_one = low(rms_scale(tokens_seq, attn_gain))
    projected = jnp.einsum('sd,kde->kse', normed_one, qkv_weight, precision=highest) + qkv_bias.reshape(3, 1, HEADS * HEAD_DIM)
    projected = low(low_back(projected)).reshape(3, SEQ, HEADS, HEAD_DIM)
    cosine, sine_table = rope_tables(SEQ, HEAD_DIM)
    query_rows = low(rotate(projected[0], cosine, sine_table))
    key_rows = low(rotate(projected[1], cosine, sine_table))
    value_rows = projected[2]
    places = jnp.arange(SEQ, dtype=jnp.int32)
    allowed = (places[None, :] <= places[:, None]) | (places[None, :] < prefix_value)
    scores = low_back(HEAD_DIM ** (-0.5) * jnp.einsum('qhd,khd->hqk', query_rows, key_rows, precision=highest))
    scores = jnp.where(allowed[None], scores, -1000000000.0)
    probs_low = low(jax.nn.softmax(scores, axis=-1))
    attended = jnp.einsum('hqk,khd->qhd', probs_low, value_rows, precision=highest).reshape(SEQ, HEADS * HEAD_DIM)
    attended = low(low_back(attended))
    hidden_res = tokens_seq + low_back(jnp.dot(attended, out_weight, precision=highest))
    normed_two = low(rms_scale(hidden_res, ffn_gain))
    router_probs = jax.nn.softmax(jnp.dot(normed_two, router_weight, precision=highest), axis=-1)
    gate_values = jnp.take_along_axis(router_probs, ids_seq, axis=1)
    slot_room = N_CTX * CAP
    slot_index, slot_owner = dispatch(ids_seq, EXPERTS, slot_room)
    padded_two = jnp.concatenate([normed_two, jnp.zeros((1, D), jnp.float32)], axis=0)
    expert_rows = padded_two[slot_owner].reshape(EXPERTS, slot_room, D)
    gate_pre = low_back(jnp.einsum('ecd,edf->ecf', expert_rows, expert_gate, precision=highest))
    up_pre = low_back(jnp.einsum('ecd,edf->ecf', expert_rows, expert_up, precision=highest))
    expert_act = low(low_back(jax.nn.silu(gate_pre) * up_pre))
    expert_res = low_back(jnp.einsum('ecf,efd->ecd', expert_act, expert_down, precision=highest)).reshape(EXPERTS * slot_room, D)
    picked = expert_res[slot_index].reshape(SEQ, TOPK, D)
    mixture = jnp.einsum('sk,skd->sd', gate_values, picked, precision=highest)
    shared_pre = low_back(jnp.dot(normed_two, shared_gate, precision=highest))
    shared_lin = low_back(jnp.dot(normed_two, shared_up, precision=highest))
    shared_act = low(low_back(jax.nn.silu(shared_pre) * shared_lin))
    shared_res = low_back(jnp.dot(shared_act, shared_down, precision=highest))
    switch = jax.nn.sigmoid(jnp.dot(normed_two, shared_switch, precision=highest))
    return hidden_res + mixture + switch[:, None] * shared_res

def reference(tokens_in, cotangent, expert_ids, prefix_len, attn_gain, qkv_weight, qkv_bias, out_weight, ffn_gain, router_weight, expert_gate, expert_up, expert_down, shared_gate, shared_up, shared_down, shared_switch):
    params = tuple((weight_arg.astype(jnp.float32) for weight_arg in (attn_gain, qkv_weight, qkv_bias, out_weight, ffn_gain, router_weight, expert_gate, expert_up, expert_down, shared_gate, shared_up, shared_down, shared_switch)))
    sequences = tokens_in.astype(jnp.float32).reshape(MICRO * BATCH, SEQ, D)
    id_rows = expert_ids.reshape(MICRO * BATCH, SEQ, TOPK).astype(jnp.int32)
    prefix_rows = prefix_len.reshape(MICRO * BATCH).astype(jnp.int32)

    def forward(inputs, weights):

        def one_sequence(packed):
            return sequence_forward(weights, packed[0], packed[1], packed[2])
        return lax.map(jax.checkpoint(one_sequence), (inputs, id_rows, prefix_rows))
    layer_out, pull_back = jax.vjp(forward, sequences, params)
    tokens_grad, param_grads = pull_back(cotangent.astype(jnp.float32).reshape(MICRO * BATCH, SEQ, D))
    return (layer_out.reshape(MICRO, BATCH, SEQ, D).astype(jnp.bfloat16), tokens_grad.reshape(MICRO, BATCH, SEQ, D), param_grads[0], param_grads[1], param_grads[2], param_grads[3], param_grads[4], param_grads[5], param_grads[6], param_grads[7], param_grads[8], param_grads[9], param_grads[10], param_grads[11], param_grads[12])
```

```python
import jax
import jax.numpy as jnp
import numpy as np
from jax import lax
from jax.sharding import PartitionSpec as P

epsilon = 1e-06
rope_base = 1000000.0
highest = lax.Precision.HIGHEST
f32 = jnp.float32
bf16 = jnp.bfloat16


def rms_scale(values, gain_vec):
    factor = lax.rsqrt(jnp.mean(values * values, axis=-1, keepdims=True) + epsilon)
    return values * factor * gain_vec


def rope_tables(length, head_dim):
    half_dim = head_dim // 2
    frequency = rope_base ** (-(np.arange(half_dim) * 2.0) / head_dim)
    places = np.arange(length)[:, None] * frequency[None, :]
    return jnp.asarray(np.cos(places), f32), jnp.asarray(np.sin(places), f32)


def rotate(values, cosine, sine_table):
    half_dim = values.shape[-1] // 2
    first_half = values[..., :half_dim]
    second_half = values[..., half_dim:]
    return jnp.concatenate(
        [
            first_half * cosine - second_half * sine_table,
            second_half * cosine + first_half * sine_table,
        ],
        axis=-1,
    )


def dot(left, right):
    return jnp.dot(left, right, preferred_element_type=f32)


def dot_rows(left, right):
    return lax.dot_general(left, right, (((0,), (0,)), ((), ())), preferred_element_type=f32)


def dot_cols(left, right):
    return lax.dot_general(left, right, (((1,), (1,)), ((), ())), preferred_element_type=f32)


def swap(values, axis, bit):
    count = lax.axis_size(axis)
    return lax.ppermute(values, axis, [(i, i ^ bit) for i in range(count)])


def pick(values, place, axis):
    return lax.dynamic_index_in_dim(values, place, axis, keepdims=False)


def sum_tp(terms):
    count = lax.axis_size("tp")
    place = lax.axis_index("tp")
    bit = 1
    while bit < count:
        pairs = terms.reshape((terms.shape[0] // 2, 2) + terms.shape[1:])
        low = (place // bit) % 2
        sent = pick(pairs, 1 - low, 1).astype(bf16)
        terms = pick(pairs, low, 1).astype(f32) + swap(sent, "tp", bit).astype(f32)
        bit *= 2
    return terms[0]


def gather_tp(block):
    count = lax.axis_size("tp")
    place = lax.axis_index("tp")
    held = block[None]
    bit = count // 2
    while bit >= 1:
        other = swap(held, "tp", bit)
        high = (place // bit) % 2
        held = jnp.where(
            high == 0, jnp.stack([held, other], 1), jnp.stack([other, held], 1)
        ).reshape((held.shape[0] * 2,) + block.shape)
        bit //= 2
    return held.reshape((count * block.shape[0],) + block.shape[1:])


def pad_to(values, axis, size):
    room = [(0, 0)] * values.ndim
    room[axis] = (0, size - values.shape[axis])
    return jnp.pad(values, room)


def round_up(size):
    return -(-size // 128) * 128


def body(
    tokens_in,
    cotangent,
    expert_ids,
    prefix_len,
    attn_gain,
    qkv_weight,
    qkv_bias,
    out_weight,
    ffn_gain,
    router_weight,
    expert_gate,
    expert_up,
    expert_down,
    shared_gate,
    shared_up,
    shared_down,
    shared_switch,
):
    n_sh, n_ctx, n_tp = lax.axis_size("shard"), lax.axis_size("ctx"), lax.axis_size("tp")
    my_sh, my_ctx, my_tp = lax.axis_index("shard"), lax.axis_index("ctx"), lax.axis_index("tp")
    micro, _, rows, width = tokens_in.shape
    picks = expert_ids.shape[-1]
    tok = micro * rows
    part = tok // n_tp
    total = n_sh * tok
    length = rows * n_ctx
    depth = qkv_weight.shape[1]
    own = width // (n_sh * n_ctx)
    local_heads, head_dim = qkv_bias.shape[1:]
    group_heads = local_heads // n_ctx
    group = group_heads * head_dim
    experts, _, hidden = expert_gate.shape
    shared_hidden = shared_gate.shape[1]
    score_scale = head_dim ** (-0.5)
    per, cut = (experts // n_sh, 1) if n_sh <= experts else (1, n_sh // experts)
    unit, share = hidden // cut, shared_hidden // n_sh
    unit_pad, share_pad = round_up(unit), round_up(share)
    block = per * unit_pad + share_pad

    inputs = tokens_in.reshape(tok, width)
    upstream = cotangent.reshape(tok, width)
    ids = expert_ids.reshape(tok, picks)

    def mine(values):
        return lax.dynamic_slice_in_dim(values, my_tp * part, part, 0)

    small = jnp.concatenate(
        [
            attn_gain,
            ffn_gain,
            shared_switch,
            router_weight.T.reshape(-1),
            ids.astype(bf16).reshape(-1),
        ]
    )
    small = lax.all_gather(small, "shard", axis=0, tiled=False)
    first_gain = small[:, :depth].reshape(width).astype(f32)
    second_gain = small[:, depth : 2 * depth].reshape(width).astype(f32)
    switch_vec = small[:, 2 * depth : 3 * depth].reshape(width)
    router_full = (
        small[:, 3 * depth : (3 + experts) * depth]
        .reshape(n_sh, experts, depth)
        .transpose(0, 2, 1)
        .reshape(width, experts)
    )
    ids_all = small[:, (3 + experts) * depth :].reshape(total, picks).astype(jnp.int32)

    qkv_local = (
        qkv_weight.reshape(3, depth, n_ctx, group).transpose(1, 2, 0, 3).reshape(depth, -1)
    )
    qkv_full = lax.all_gather(qkv_local, "shard", axis=0, tiled=True)
    bias_row = qkv_bias.reshape(3, n_ctx, group).transpose(1, 0, 2).reshape(1, -1).astype(f32)
    out_full = lax.all_gather(out_weight, "shard", axis=1, tiled=True)

    def spread_in(expert_part, shared_part):
        one = (
            expert_part.reshape(experts, depth, cut, unit)
            .transpose(0, 2, 1, 3)
            .reshape(n_sh, per, depth, unit)
        )
        one = pad_to(one, 3, unit_pad).transpose(0, 2, 1, 3).reshape(n_sh, depth, per * unit_pad)
        two = pad_to(shared_part.reshape(depth, n_sh, share).transpose(1, 0, 2), 2, share_pad)
        return [one, two]

    gate_up = jnp.concatenate(
        spread_in(expert_gate, shared_gate) + spread_in(expert_up, shared_up), axis=2
    )
    gate_up = lax.all_to_all(gate_up, "shard", 0, 0, tiled=True).reshape(width, 2 * block)
    down = jnp.concatenate(
        [
            pad_to(expert_down.reshape(n_sh, per, unit, depth), 2, unit_pad).reshape(
                n_sh, per * unit_pad, depth
            ),
            pad_to(shared_down.reshape(n_sh, share, depth), 1, share_pad),
        ],
        axis=1,
    )
    down = lax.all_to_all(down, "shard", 0, 0, tiled=True).transpose(1, 0, 2).reshape(block, width)
    up_all = lax.all_gather(mine(upstream), ("shard", "tp"), axis=0, tiled=True)

    normed_one = rms_scale(inputs.astype(f32), first_gain).astype(bf16)
    projected = (dot(normed_one, qkv_full) + bias_row).astype(bf16)
    by_heads = lax.all_to_all(
        projected.reshape(tok, n_ctx, 3 * group).transpose(1, 0, 2), "ctx", 0, 0, tiled=True
    )
    by_heads = (
        by_heads.reshape(n_ctx, micro, rows, 3, group_heads, head_dim)
        .transpose(3, 1, 4, 0, 2, 5)
        .reshape(3, micro, group_heads, length, head_dim)
    )
    cosine, sine_table = rope_tables(length, head_dim)
    query_rows = rotate(by_heads[0].astype(f32), cosine, sine_table).astype(bf16)
    key_rows = rotate(by_heads[1].astype(f32), cosine, sine_table).astype(bf16)
    value_rows = by_heads[2]
    places = jnp.arange(length, dtype=jnp.int32)
    allowed = (places[None, :] <= places[:, None])[None] | (
        places[None, None, :] < prefix_len.reshape(micro, 1, 1)
    )
    scores = (
        jnp.einsum("mhqd,mhkd->mhqk", query_rows, key_rows, preferred_element_type=f32)
        * score_scale
    )
    scores = jnp.where(allowed[:, None], scores, -1000000000.0)
    raised = jnp.exp(scores - jnp.max(scores, axis=-1, keepdims=True))
    probs = raised / jnp.sum(raised, axis=-1, keepdims=True)
    probs_low = probs.astype(bf16)
    attended = jnp.einsum(
        "mhqk,mhkd->mhqd", probs_low, value_rows, preferred_element_type=f32
    ).astype(bf16)
    attended = (
        attended.reshape(micro, group_heads, n_ctx, rows, head_dim)
        .transpose(2, 0, 3, 1, 4)
        .reshape(n_ctx, tok, group)
    )
    head_rows = (
        lax.all_to_all(attended, "ctx", 0, 0, tiled=True)
        .transpose(1, 0, 2)
        .reshape(tok, n_ctx * group)
    )
    attn_total = sum_tp(dot(head_rows, out_full).reshape(n_tp, part, width))

    my_inputs = mine(inputs).astype(f32)
    my_up = mine(upstream).astype(f32)
    hidden_res = my_inputs + attn_total
    second_float, second_pull = jax.vjp(rms_scale, hidden_res, second_gain)
    my_normed = second_float.astype(bf16)
    normed_two = lax.all_gather(my_normed, ("shard", "tp"), axis=0, tiled=True)

    routing = jnp.concatenate([router_full, switch_vec[:, None]], axis=1)

    def route(values):
        logits = dot(values, routing)
        return jax.nn.softmax(logits[:, :experts], axis=-1), jax.nn.sigmoid(logits[:, experts])

    probs_all, switch_all = route(normed_two)
    first_expert = my_sh * per // cut
    gates, names = [], []
    for k in range(per):
        named = jnp.any(ids_all == first_expert + k, axis=1)
        chosen = lax.dynamic_index_in_dim(probs_all, first_expert + k, 1, keepdims=False)
        names.append(named)
        gates.append(jnp.where(named, chosen, 0.0))
    gates.append(switch_all)
    column = lax.broadcasted_iota(jnp.int32, (total, block), 1)
    gate_wide = jnp.broadcast_to(gates[-1][:, None], (total, block))
    for k in reversed(range(per)):
        gate_wide = jnp.where(column < (k + 1) * unit_pad, gates[k][:, None], gate_wide)

    pre = dot(normed_two, gate_up)
    pre_gate, pre_up = pre[:, :block], pre[:, block:]
    sigma = jax.nn.sigmoid(pre_gate)
    silu = pre_gate * sigma
    act = silu * pre_up
    act_low = (gate_wide * act).astype(bf16)
    back = dot_cols(up_all, down)
    act_grad = gate_wide * back
    pre_grad = jnp.concatenate(
        [
            (act_grad * pre_up * (sigma + silu * (1.0 - sigma))).astype(bf16),
            (act_grad * silu).astype(bf16),
        ],
        axis=1,
    )
    mixed = dot(act_low, down).astype(bf16)
    product = act * back
    lane = lax.broadcasted_iota(jnp.int32, (1, 128), 1)
    gate_terms = jnp.zeros((total, 128), f32)
    for k in range(per):
        term = jnp.sum(product[:, k * unit_pad : (k + 1) * unit_pad], axis=1)
        term = jnp.where(names[k], term, 0.0)
        gate_terms = gate_terms + jnp.where(lane == first_expert + k, term[:, None], 0.0)
    term = jnp.sum(product[:, per * unit_pad :], axis=1)
    gate_terms = gate_terms + jnp.where(lane == experts, term[:, None], 0.0)
    gate_terms = lax.psum_scatter(
        gate_terms.astype(bf16), ("shard", "tp"), scatter_dimension=0, tiled=True
    ).astype(f32)
    normed_grad = lax.psum_scatter(
        dot_cols(pre_grad, gate_up).astype(bf16),
        ("shard", "tp"),
        scatter_dimension=0,
        tiled=True,
    ).astype(f32)
    ffn_total = lax.psum_scatter(
        mixed, ("shard", "tp"), scatter_dimension=0, tiled=True
    ).astype(f32)
    layer_out = gather_tp((hidden_res + ffn_total).astype(bf16))

    def halves(values):
        split = values.reshape(total, n_sh, n_ctx, own)
        return (
            pick(split, 1 - my_ctx, 2).reshape(total, n_sh * own),
            pick(split, my_ctx, 2).reshape(total, n_sh * own),
        )

    up_other, up_mine = halves(up_all)
    two_other, two_mine = halves(normed_two)
    down_other = swap(dot_rows(act_low, up_other).astype(bf16), "ctx", 1)
    gate_up_other = swap(dot_rows(two_other, pre_grad).astype(bf16), "ctx", 1)
    down_grad = (dot_rows(act_low, up_mine) + down_other.astype(f32)).astype(bf16)
    gate_up_grad = (dot_rows(two_mine, pre_grad) + gate_up_other.astype(f32)).astype(bf16)
    down_grad = lax.all_to_all(
        down_grad.reshape(block, n_sh, own).transpose(1, 0, 2), "shard", 0, 0, tiled=True
    ).astype(f32)
    gate_up_grad = lax.all_to_all(
        gate_up_grad.reshape(n_sh, own, 2 * block), "shard", 0, 0, tiled=True
    ).astype(f32)

    def spread_out(grads):
        one = grads[:, :, : per * unit_pad].reshape(n_sh, own, per, unit_pad)[..., :unit]
        one = (
            one.transpose(0, 2, 1, 3)
            .reshape(experts, cut, own, unit)
            .transpose(0, 2, 1, 3)
            .reshape(experts, own, hidden)
        )
        two = grads[:, :, per * unit_pad : per * unit_pad + share]
        return one, two.transpose(1, 0, 2).reshape(own, shared_hidden)

    expert_gate_grad, shared_gate_grad = spread_out(gate_up_grad[:, :, :block])
    expert_up_grad, shared_up_grad = spread_out(gate_up_grad[:, :, block:])
    expert_down_grad = (
        down_grad[:, : per * unit_pad]
        .reshape(n_sh, per, unit_pad, own)[:, :, :unit]
        .reshape(experts, hidden, own)
    )
    shared_down_grad = down_grad[:, per * unit_pad :][:, :share].reshape(shared_hidden, own)

    my_probs, my_switch = route(my_normed)
    prob_grads = gate_terms[:, :experts]
    logit_grads = my_probs * (
        prob_grads - jnp.sum(my_probs * prob_grads, axis=-1, keepdims=True)
    )
    switch_pre_grad = gate_terms[:, experts] * my_switch * (1.0 - my_switch)
    route_grads = jnp.concatenate([logit_grads, switch_pre_grad[:, None]], axis=1)
    normed_float = my_normed.astype(f32)
    routing_grad = lax.dot_general(
        route_grads, normed_float, (((0,), (0,)), ((), ())), precision=highest
    )
    normed_grad = normed_grad + lax.dot_general(
        route_grads, routing.astype(f32), (((1,), (1,)), ((), ())), precision=highest
    )
    hidden_norm_grad, ffn_gain_grad = second_pull(normed_grad)
    hidden_grad = my_up + hidden_norm_grad
    early = lax.psum(
        jnp.concatenate([routing_grad, ffn_gain_grad[None]], axis=0), ("shard", "ctx", "tp")
    )

    branch_low = gather_tp(hidden_grad.astype(bf16))
    out_weight_grad = dot_rows(head_rows, branch_low).astype(bf16)
    out_weight_grad = lax.psum_scatter(out_weight_grad, "shard", scatter_dimension=1, tiled=True)
    out_weight_grad = lax.psum_scatter(
        out_weight_grad, "ctx", scatter_dimension=1, tiled=True
    ).astype(f32)
    head_grad = dot_cols(branch_low, out_full).astype(bf16)
    head_grad = lax.all_to_all(
        head_grad.reshape(tok, n_ctx, group).transpose(1, 0, 2), "ctx", 0, 0, tiled=True
    )
    head_grad = (
        head_grad.reshape(n_ctx, micro, rows, group_heads, head_dim)
        .transpose(1, 3, 0, 2, 4)
        .reshape(micro, group_heads, length, head_dim)
    )
    prob_grad = jnp.einsum("mhqd,mhkd->mhqk", head_grad, value_rows, preferred_element_type=f32)
    value_grad = jnp.einsum("mhqk,mhqd->mhkd", probs_low, head_grad, preferred_element_type=f32)
    score_low = (
        probs * (prob_grad - jnp.sum(probs * prob_grad, axis=-1, keepdims=True))
    ).astype(bf16)
    query_grad = (
        jnp.einsum("mhqk,mhkd->mhqd", score_low, key_rows, preferred_element_type=f32)
        * score_scale
    )
    key_grad = (
        jnp.einsum("mhqk,mhqd->mhkd", score_low, query_rows, preferred_element_type=f32)
        * score_scale
    )
    stacked = jnp.stack(
        [
            rotate(query_grad, cosine, -sine_table),
            rotate(key_grad, cosine, -sine_table),
            value_grad,
        ]
    ).astype(bf16)
    stacked = (
        stacked.reshape(3, micro, group_heads, n_ctx, rows, head_dim)
        .transpose(3, 1, 4, 0, 2, 5)
        .reshape(n_ctx, tok, 3 * group)
    )
    proj_grad = (
        lax.all_to_all(stacked, "ctx", 0, 0, tiled=True)
        .transpose(1, 0, 2)
        .reshape(tok, n_ctx * 3 * group)
    )
    qkv_grad = dot_rows(normed_one, proj_grad).astype(bf16)
    qkv_grad = lax.psum_scatter(qkv_grad, "shard", scatter_dimension=0, tiled=True)
    qkv_grad = lax.psum_scatter(qkv_grad, "ctx", scatter_dimension=0, tiled=True).astype(f32)
    qkv_grad = (
        qkv_grad.reshape(own, n_ctx, 3, group).transpose(2, 0, 1, 3).reshape(3, own, n_ctx * group)
    )
    bias_grad = jnp.sum(proj_grad.astype(f32), axis=0)
    normed_one_grad = sum_tp(dot_cols(proj_grad, qkv_full).reshape(n_tp, part, width))
    _, first_pull = jax.vjp(rms_scale, my_inputs, first_gain)
    input_norm_grad, attn_gain_grad = first_pull(normed_one_grad)
    tokens_grad = gather_tp((hidden_grad + input_norm_grad).astype(bf16)).astype(f32)

    bias_spread = jnp.where(
        jnp.arange(n_tp)[:, None] == my_tp, bias_grad[None], 0.0
    ).reshape(-1)
    late = lax.psum(jnp.concatenate([attn_gain_grad, bias_spread]), ("shard", "ctx", "tp"))
    late_bias = lax.dynamic_slice_in_dim(late[width:], my_tp * bias_grad.size, bias_grad.size)
    late_bias = (
        late_bias.reshape(n_ctx, 3, group_heads, head_dim)
        .transpose(1, 0, 2, 3)
        .reshape(3, local_heads, head_dim)
    )
    place = my_sh * n_ctx + my_ctx
    early = lax.dynamic_slice_in_dim(early, place * own, own, 1)
    bias_own = head_dim // (n_sh * n_ctx)
    shape = (micro, 1, rows, width)
    return (
        layer_out.reshape(shape),
        tokens_grad.reshape(shape),
        lax.dynamic_slice_in_dim(late[:width], place * own, own),
        qkv_grad,
        lax.dynamic_slice_in_dim(late_bias, place * bias_own, bias_own, 2),
        out_weight_grad,
        early[experts + 1],
        early[:experts].T,
        expert_gate_grad,
        expert_up_grad,
        expert_down_grad,
        shared_gate_grad,
        shared_up_grad,
        shared_down_grad,
        early[experts],
    )


def solution(mesh):
    in_specs = (
        P(None, "shard", "ctx", None),
        P(None, "shard", "ctx", None),
        P(None, "shard", "ctx", None),
        P(None, "shard"),
        P("shard"),
        P(None, "shard", "tp"),
        P(None, "tp", None),
        P("tp", "shard"),
        P("shard"),
        P("shard", None),
        P(None, "shard", "tp"),
        P(None, "shard", "tp"),
        P(None, "tp", "shard"),
        P("shard", "tp"),
        P("shard", "tp"),
        P("tp", "shard"),
        P("shard"),
    )
    out_specs = (
        P(None, "shard", "ctx", None),
        P(None, "shard", "ctx", None),
        P(("shard", "ctx")),
        P(None, ("shard", "ctx"), "tp"),
        P(None, "tp", ("shard", "ctx")),
        P("tp", ("shard", "ctx")),
        P(("shard", "ctx")),
        P(("shard", "ctx"), None),
        P(None, ("shard", "ctx"), "tp"),
        P(None, ("shard", "ctx"), "tp"),
        P(None, "tp", ("shard", "ctx")),
        P(("shard", "ctx"), "tp"),
        P(("shard", "ctx"), "tp"),
        P("tp", ("shard", "ctx")),
        P(("shard", "ctx")),
    )
    return jax.shard_map(body, mesh=mesh, in_specs=in_specs, out_specs=out_specs, check_vma=False)
```

```python
import functools

import jax
import jax.numpy as jnp
import numpy as np
from jax import lax
from jax.experimental import pallas as pl
from jax.experimental.pallas import tpu as pltpu
from jax.sharding import PartitionSpec as P

epsilon = 1e-06
rope_base = 1000000.0
highest = lax.Precision.HIGHEST
f32 = jnp.float32
bf16 = jnp.bfloat16


def rms_scale(values, gain_vec):
    factor = lax.rsqrt(jnp.mean(values * values, axis=-1, keepdims=True) + epsilon)
    return values * factor * gain_vec


def rope_tables(length, head_dim):
    half_dim = head_dim // 2
    frequency = rope_base ** (-(np.arange(half_dim) * 2.0) / head_dim)
    places = np.arange(length)[:, None] * frequency[None, :]
    return jnp.asarray(np.cos(places), f32), jnp.asarray(np.sin(places), f32)


def rotate(values, cosine, sine_table):
    half_dim = values.shape[-1] // 2
    first_half = values[..., :half_dim]
    second_half = values[..., half_dim:]
    return jnp.concatenate(
        [
            first_half * cosine - second_half * sine_table,
            second_half * cosine + first_half * sine_table,
        ],
        axis=-1,
    )


def dot(left, right):
    return jnp.dot(left, right, preferred_element_type=f32)


def dot_rows(left, right):
    return lax.dot_general(left, right, (((0,), (0,)), ((), ())), preferred_element_type=f32)


def dot_cols(left, right):
    return lax.dot_general(left, right, (((1,), (1,)), ((), ())), preferred_element_type=f32)


def swap(values, axis, bit):
    count = lax.axis_size(axis)
    return lax.ppermute(values, axis, [(i, i ^ bit) for i in range(count)])


def pick(values, place, axis):
    return lax.dynamic_index_in_dim(values, place, axis, keepdims=False)


def sum_tp(terms):
    count = lax.axis_size("tp")
    place = lax.axis_index("tp")
    bit = 1
    while bit < count:
        pairs = terms.reshape((terms.shape[0] // 2, 2) + terms.shape[1:])
        low = (place // bit) % 2
        sent = pick(pairs, 1 - low, 1).astype(bf16)
        terms = pick(pairs, low, 1).astype(f32) + swap(sent, "tp", bit).astype(f32)
        bit *= 2
    return terms[0]


def gather_tp(block):
    count = lax.axis_size("tp")
    place = lax.axis_index("tp")
    held = block[None]
    bit = count // 2
    while bit >= 1:
        other = swap(held, "tp", bit)
        high = (place // bit) % 2
        held = jnp.where(
            high == 0, jnp.stack([held, other], 1), jnp.stack([other, held], 1)
        ).reshape((held.shape[0] * 2,) + block.shape)
        bit //= 2
    return held.reshape((count * block.shape[0],) + block.shape[1:])


def round_up(size):
    return -(-size // 128) * 128


def pad_to(values, axis, size):
    room = [(0, 0)] * values.ndim
    room[axis] = (0, size - values.shape[axis])
    return jnp.pad(values, room)


def tie(values, *after):
    return lax.optimization_barrier((values,) + after)[0]


def core_groups():
    n_sh, half = lax.axis_size("shard"), lax.axis_size("tp") // 2
    return [
        [s * 2 * half + z * 2 + core for s in range(n_sh) for z in range(half)]
        for core in range(2)
    ]


def exchange(values):
    return lax.all_to_all(
        values, ("shard", "tp"), 0, 0, tiled=True, axis_index_groups=core_groups()
    )


def gather_core(block):
    peers = lax.axis_size("shard") * lax.axis_size("tp") // 2
    return exchange(jnp.broadcast_to(block[None], (peers,) + block.shape))


def both_cores(own):
    return jnp.concatenate([own, swap(own, "tp", 1)]).reshape(-1, own.shape[-1])


def sum_core(other, make_own):
    arrived = swap(other, "tp", 1)
    return (make_own().astype(f32) + arrived.astype(f32)).astype(bf16)


def sum_shard_z(own):
    half = lax.axis_size("tp") // 2
    z = lax.axis_index("tp") // 2
    own = lax.all_to_all(own, "shard", 0, 0, tiled=True)
    own = jnp.sum(own.reshape((-1, half) + own.shape[1:]).astype(f32), axis=0)
    return pick(own, z, 0) + swap(pick(own, 1 - z, 0).astype(bf16), "tp", 2).astype(f32)


def sum_rows_small(terms):
    n_sh, half = lax.axis_size("shard"), lax.axis_size("tp") // 2
    terms = terms[0] + swap(terms[1], "tp", 1)
    terms = terms.reshape((n_sh, half) + terms.shape[1:]).swapaxes(0, 1)
    for axis, place, scale in (
        ("tp", lax.axis_index("tp") // 2, 2),
        ("shard", lax.axis_index("shard"), 1),
    ):
        bit = 1
        while terms.shape[0] > 1:
            pairs = terms.reshape((terms.shape[0] // 2, 2) + terms.shape[1:])
            low = (place // bit) % 2
            terms = pick(pairs, low, 1) + swap(pick(pairs, 1 - low, 1), axis, bit * scale)
            bit *= 2
        terms = terms[0]
    return terms


def sum_tp_small(terms):
    bit = 1
    while bit < lax.axis_size("tp"):
        terms = terms + swap(terms, "tp", bit)
        bit *= 2
    return terms


def others(values, axis):
    count = lax.axis_size(axis)
    return [values[0]] + [swap(values[k], axis, k) for k in range(1, count)]


def in_order(pieces, axis):
    place = lax.axis_index(axis) ^ jnp.arange(len(pieces), dtype=jnp.int32)
    return jnp.take(jnp.stack(pieces), place, axis=0)


def place_kernel(count, place, rows, *refs):
    out = refs[-1]
    size = rows.shape[0] // count
    room = round_up(size)
    for k in range(count):
        part = rows[k * size : (k + 1) * size]
        if room > size:
            part = jnp.concatenate(
                [part, jnp.zeros((room - size, part.shape[1]), part.dtype)], axis=0
            )
        out[k * room : (k + 1) * room, :] = part


def place_columns(values, count, held, place, parts):
    rows, depth = values.shape
    n_sh = lax.axis_size("shard")
    chunk = depth // parts
    height = count * round_up(rows // count)
    operands = [values]
    specs = [pl.BlockSpec((rows, chunk), lambda c, at: (0, c))]
    aliases = {}
    if held is not None:
        aliases = {2: 0}
        operands.append(held)
        specs.append(pl.BlockSpec(memory_space=pl.ANY))
    return pl.pallas_call(
        functools.partial(place_kernel, count),
        grid_spec=pltpu.PrefetchScalarGridSpec(
            num_scalar_prefetch=1,
            grid=(parts,),
            in_specs=specs,
            out_specs=pl.BlockSpec((height, chunk), lambda c, at: (0, c * n_sh + at[0])),
        ),
        out_shape=jax.ShapeDtypeStruct((height, n_sh * depth), bf16),
        input_output_aliases=aliases,
        compiler_params=pltpu.CompilerParams(vmem_limit_bytes=32 * 2**20),
        cost_estimate=pl.CostEstimate(
            flops=0, bytes_accessed=4 * height * depth, transcendentals=0
        ),
    )(jnp.reshape(place, (1,)), *operands)


def unpack_kernel(place, *refs):
    count = len(refs) - 2
    one, two = refs[count:]
    first = one.shape[1]
    for step in range(count):

        @pl.when(pl.program_id(0) == step)
        def _(grads=refs[step]):
            one[0] = grads[:first].astype(f32)
            two[0] = grads[first:].astype(f32)


def unpack(pieces, place, first):
    count = len(pieces)
    units, own = pieces[0].shape

    def where(step, at):
        return (at[0] ^ step, 0, 0)

    return pl.pallas_call(
        unpack_kernel,
        grid_spec=pltpu.PrefetchScalarGridSpec(
            num_scalar_prefetch=1,
            grid=(count,),
            in_specs=[pl.BlockSpec((units, own), lambda step, at: (0, 0))] * count,
            out_specs=[
                pl.BlockSpec((1, first, own), where),
                pl.BlockSpec((1, units - first, own), where),
            ],
        ),
        out_shape=[
            jax.ShapeDtypeStruct((count, first, own), f32),
            jax.ShapeDtypeStruct((count, units - first, own), f32),
        ],
        compiler_params=pltpu.CompilerParams(vmem_limit_bytes=32 * 2**20),
        cost_estimate=pl.CostEstimate(
            flops=0, bytes_accessed=6 * count * own * units, transcendentals=0
        ),
    )(jnp.reshape(place, (1,)), *pieces)


def body(
    tokens_in,
    cotangent,
    expert_ids,
    prefix_len,
    attn_gain,
    qkv_weight,
    qkv_bias,
    out_weight,
    ffn_gain,
    router_weight,
    expert_gate,
    expert_up,
    expert_down,
    shared_gate,
    shared_up,
    shared_down,
    shared_switch,
):
    n_sh, n_ctx, n_tp = lax.axis_size("shard"), lax.axis_size("ctx"), lax.axis_size("tp")
    my_sh, my_ctx, my_tp = lax.axis_index("shard"), lax.axis_index("ctx"), lax.axis_index("tp")
    micro, _, rows, width = tokens_in.shape
    picks = expert_ids.shape[-1]
    tok = micro * rows
    part = tok // n_tp
    total = n_sh * tok
    length = rows * n_ctx
    depth = qkv_weight.shape[1]
    own = width // (n_sh * n_ctx)
    local_heads, head_dim = qkv_bias.shape[1:]
    heads_width = local_heads * head_dim
    experts, _, hidden = expert_gate.shape
    shared_hidden = shared_gate.shape[1]
    score_scale = head_dim ** (-0.5)
    per = max(experts // n_sh, 1)
    mine_first = experts * hidden // n_sh
    unit = mine_first // per
    used = mine_first + shared_hidden // n_sh
    block = round_up(used)

    inputs = tokens_in.reshape(tok, width)
    upstream = cotangent.reshape(tok, width)
    ids = expert_ids.reshape(tok, picks)

    def mine(values):
        return lax.dynamic_slice_in_dim(values, my_tp * part, part, 0)

    small = jnp.concatenate(
        [
            attn_gain,
            ffn_gain,
            shared_switch,
            router_weight.T.reshape(-1),
            ids.astype(bf16).reshape(-1),
        ]
    )
    small = in_order(others([small] * n_sh, "shard"), "shard")
    first_gain = small[:, :depth].reshape(width).astype(f32)
    second_gain = small[:, depth : 2 * depth].reshape(width).astype(f32)
    switch_vec = small[:, 2 * depth : 3 * depth].reshape(width)
    router_full = (
        small[:, 3 * depth : (3 + experts) * depth]
        .reshape(n_sh, experts, depth)
        .transpose(0, 2, 1)
        .reshape(width, experts)
    )
    ids_all = small[:, (3 + experts) * depth :].reshape(n_sh * n_tp // 2, 2, part, picks)
    core = my_tp % 2
    ids_all = jnp.stack([pick(ids_all, core, 1), pick(ids_all, 1 - core, 1)])
    ids_all = ids_all.reshape(total, picks).astype(jnp.int32)

    qkv_local = qkv_weight.transpose(1, 0, 2).reshape(depth, 3 * heads_width)
    qkv_full = lax.all_gather(qkv_local, "shard", axis=0, tiled=True)
    bias_row = qkv_bias.reshape(1, 3 * heads_width).astype(f32)
    out_full = lax.all_gather(out_weight, "shard", axis=1, tiled=True)

    parts = n_ctx if own % 128 == 0 else 1
    chunk = depth // parts

    def to_parts(values):
        shape = values.shape[:-1]
        values = values.reshape(shape + (n_sh, parts, chunk))
        return values.swapaxes(-3, -2).reshape(shape + (width,))

    def from_parts(values):
        shape = values.shape[:-1]
        values = values.reshape(shape + (parts, n_sh, chunk))
        return values.swapaxes(-3, -2).reshape(shape + (width,))

    gate_up_local = (
        expert_gate.transpose(0, 2, 1).reshape(n_sh, mine_first, depth),
        shared_gate.T.reshape(n_sh, used - mine_first, depth),
        expert_up.transpose(0, 2, 1).reshape(n_sh, mine_first, depth),
        shared_up.T.reshape(n_sh, used - mine_first, depth),
    )
    down_local = (
        expert_down.reshape(n_sh, mine_first, depth),
        shared_down.reshape(n_sh, used - mine_first, depth),
    )

    def fetch(values, k, after):
        values = jnp.concatenate([pick(v, my_sh ^ k, 0) for v in values])
        return swap(tie(values, after), "shard", k) if k else values

    def fetch_gate_up(which, after, held):
        for k in which:
            values = fetch(gate_up_local, k, after)
            held = place_columns(values, 2, held, my_sh ^ k, parts)
        return held

    near, far = range(n_sh // 2 + 1), range(n_sh // 2 + 1, n_sh)

    normed_one = rms_scale(inputs.astype(f32), first_gain).astype(bf16)
    projected = (dot(normed_one, qkv_full) + bias_row).astype(bf16)

    def heads(values):
        return values.reshape(micro, rows, local_heads, head_dim).transpose(0, 2, 1, 3)

    def flat(values):
        return values.transpose(0, 2, 1, 3).reshape(tok, heads_width)

    cosine, sine_table = rope_tables(length, head_dim)
    cosine = lax.dynamic_slice_in_dim(cosine, my_ctx * rows, rows, 0)
    sine_table = lax.dynamic_slice_in_dim(sine_table, my_ctx * rows, rows, 0)
    query_rows, key_rows = (
        rotate(
            heads(projected[:, k * heads_width : (k + 1) * heads_width]).astype(f32),
            cosine,
            sine_table,
        ).astype(bf16)
        for k in range(2)
    )
    value_rows = heads(projected[:, 2 * heads_width :])
    own_rows = jnp.stack([key_rows, value_rows])
    other_rows = swap(own_rows, "ctx", 1)
    gate_up = fetch_gate_up(near, qkv_full, None)
    key_all, value_all = jnp.concatenate([own_rows, other_rows], axis=3)
    steps = jnp.arange(rows, dtype=jnp.int32)
    query_at = my_ctx * rows + steps
    key_at = jnp.concatenate([query_at, (1 - my_ctx) * rows + steps])
    allowed = (key_at[None, :] <= query_at[:, None])[None] | (
        key_at[None, None, :] < prefix_len.reshape(micro, 1, 1)
    )
    scores = (
        jnp.einsum("mhqd,mhkd->mhqk", query_rows, key_all, preferred_element_type=f32)
        * score_scale
    )
    scores = jnp.where(allowed[:, None], scores, -1000000000.0)
    raised = jnp.exp(scores - jnp.max(scores, axis=-1, keepdims=True))
    probs = raised / jnp.sum(raised, axis=-1, keepdims=True)
    probs_low = probs.astype(bf16)
    head_rows = flat(
        jnp.einsum("mhqk,mhkd->mhqd", probs_low, value_all, preferred_element_type=f32).astype(
            bf16
        )
    )
    head_rows = tie(head_rows, gate_up)
    gate_up = fetch_gate_up(far, other_rows, gate_up)
    down_pieces = [fetch(down_local, k, head_rows) for k in range(n_sh)]
    attn_total = sum_tp(dot(head_rows, out_full).reshape(n_tp, part, width))

    my_inputs = mine(inputs).astype(f32)
    my_up = mine(upstream).astype(f32)
    hidden_res = my_inputs + tie(attn_total, gate_up, *down_pieces)
    second_float, second_pull = jax.vjp(rms_scale, hidden_res, second_gain)
    my_normed = second_float.astype(bf16)
    normed_two = both_cores(gather_core(to_parts(my_normed)))
    up_core = gather_core(tie(to_parts(mine(upstream)), my_normed))
    routing = jnp.concatenate([router_full, switch_vec[:, None]], axis=1)

    def route(values, weights):
        logits = dot(values, weights)
        return jax.nn.softmax(logits[:, :experts], axis=-1), jax.nn.sigmoid(logits[:, experts])

    probs_all, switch_all = route(normed_two, to_parts(routing.T).T)
    first_expert = my_sh * experts // n_sh
    gates, names = [], []
    for k in range(per):
        named = jnp.any(ids_all == first_expert + k, axis=1)
        chosen = lax.dynamic_index_in_dim(probs_all, first_expert + k, 1, keepdims=False)
        names.append(named)
        gates.append(jnp.where(named, chosen, 0.0))
    gates.append(switch_all)
    column = lax.broadcasted_iota(jnp.int32, (total, block), 1)
    gate_wide = jnp.broadcast_to(gates[-1][:, None], (total, block))
    for k in reversed(range(per)):
        gate_wide = jnp.where(column < (k + 1) * unit, gates[k][:, None], gate_wide)

    pre = dot_cols(normed_two, gate_up)
    pre_gate, pre_up = pre[:, :block], pre[:, block:]
    sigma = jax.nn.sigmoid(pre_gate)
    silu = pre_gate * sigma
    act = silu * pre_up
    act_low = (gate_wide * act).astype(bf16)
    up_all = both_cores(tie(up_core, pre))
    down = None
    for k in range(n_sh):
        down = place_columns(tie(down_pieces[k], pre), 1, down, my_sh ^ k, parts)
    back = dot_cols(up_all, down)
    act_grad = gate_wide * back
    pre_grad = jnp.concatenate(
        [
            (act_grad * pre_up * (sigma + silu * (1.0 - sigma))).astype(bf16),
            (act_grad * silu).astype(bf16),
        ],
        axis=1,
    )
    product = act * back
    lane = lax.broadcasted_iota(jnp.int32, (1, 128), 1)
    gate_terms = jnp.zeros((total, 128), f32)
    for k in range(per + 1):
        inside = (column >= k * unit) & (column < ((k + 1) * unit if k < per else block))
        term = jnp.sum(jnp.where(inside, product, 0.0), axis=1)
        if k < per:
            term = jnp.where(names[k], term, 0.0)
        at = first_expert + k if k < per else experts
        gate_terms = gate_terms + jnp.where(lane == at, term[:, None], 0.0)
    half = total // 2
    peers = n_sh * n_tp // 2

    def grad_whole(units, values):
        if parts == n_ctx:
            span = width // n_ctx
            return jnp.stack(
                [
                    dot_rows(units, values[:, c * span : (c + 1) * span]).astype(bf16)
                    for c in range(n_ctx)
                ]
            )
        whole = dot_rows(units, values).astype(bf16)
        return whole.reshape(used, n_sh, n_ctx, own).transpose(2, 0, 1, 3).reshape(n_ctx, used, -1)

    def sum_ctx_parts(whole):
        return lax.psum_scatter(whole, "ctx", scatter_dimension=0, tiled=True)[0]

    down_whole = grad_whole(act_low[:, :used], up_all)
    down_piece = sum_ctx_parts(down_whole)
    pre_grad = tie(pre_grad, down_whole)

    def spread(values):
        return values.astype(bf16).reshape(peers, part, values.shape[-1])

    gate_terms = sum_rows_small(gate_terms.reshape(2, peers, part, gate_terms.shape[-1]))
    own_grad = sum_core(
        spread(dot(pre_grad[half:], gate_up)),
        lambda: dot(pre_grad[:half], gate_up).reshape(peers, part, width),
    )
    pre_grad = tie(pre_grad, own_grad)
    gate_whole = grad_whole(pre_grad[:, :used], normed_two)
    up_whole = grad_whole(pre_grad[:, block : block + used], normed_two)
    cut_at = used // 2
    gate_first = sum_ctx_parts(gate_whole[:, :cut_at])
    act_low = tie(act_low, up_whole)
    own_mixed = sum_core(
        spread(dot(act_low[half:], down)),
        lambda: dot(act_low[:half], down).reshape(peers, part, width),
    )
    normed_grad = sum_shard_z(tie(own_grad, gate_terms))
    own_mixed = tie(own_mixed, normed_grad)
    normed_grad = from_parts(tie(normed_grad, gate_whole, up_whole, own_mixed))
    ffn_total = from_parts(sum_shard_z(own_mixed))

    def settle(piece):
        pieces = [
            lax.dynamic_slice_in_dim(piece, (my_sh ^ k) * own, own, 1) for k in range(n_sh)
        ]
        one, two = unpack(others(pieces, "shard"), my_sh, mine_first)
        return one.reshape(experts, hidden, own), two.reshape(shared_hidden, own)

    my_probs, my_switch = route(my_normed, routing)
    prob_grads = gate_terms[:, :experts]
    logit_grads = my_probs * (
        prob_grads - jnp.sum(my_probs * prob_grads, axis=-1, keepdims=True)
    )
    switch_pre_grad = gate_terms[:, experts] * my_switch * (1.0 - my_switch)
    route_grads = jnp.concatenate([logit_grads, switch_pre_grad[:, None]], axis=1)
    normed_float = my_normed.astype(f32)
    routing_grad = lax.dot_general(
        route_grads, normed_float, (((0,), (0,)), ((), ())), precision=highest
    )
    normed_grad = normed_grad + lax.dot_general(
        route_grads, routing.astype(f32), (((1,), (1,)), ((), ())), precision=highest
    )
    hidden_norm_grad, ffn_gain_grad = second_pull(normed_grad)
    hidden_grad = my_up + hidden_norm_grad

    def sum_shard(terms):
        pieces = others([pick(terms, my_sh ^ k, 0) for k in range(n_sh)], "shard")
        return sum(piece.astype(f32) for piece in pieces)

    def sum_ctx(terms):
        arrived = swap(pick(terms, 1 - my_ctx, 0).astype(bf16), "ctx", 1)
        return pick(terms, my_ctx, 0) + arrived.astype(f32)

    branch_low = gather_tp(hidden_grad.astype(bf16))
    out_weight_grad = dot_rows(head_rows, branch_low).astype(bf16)
    out_weight_grad = sum_shard(
        out_weight_grad.reshape(-1, n_sh, n_ctx * own).transpose(1, 0, 2)
    ).reshape(-1, n_ctx, own)
    out_weight_grad = sum_ctx(out_weight_grad.transpose(1, 0, 2))
    head_grad = dot_cols(branch_low, out_full).astype(bf16)
    expert_down_grad, shared_down_grad = settle(down_piece)
    my_out = (hidden_res + ffn_total).astype(bf16)
    head_grad = heads(head_grad)
    prob_grad = jnp.einsum("mhqd,mhkd->mhqk", head_grad, value_all, preferred_element_type=f32)
    value_grad = jnp.einsum("mhqk,mhqd->mhkd", probs_low, head_grad, preferred_element_type=f32)
    score_low = (
        probs * (prob_grad - jnp.sum(probs * prob_grad, axis=-1, keepdims=True))
    ).astype(bf16)
    query_grad = jnp.einsum("mhqk,mhkd->mhqd", score_low, key_all, preferred_element_type=f32)
    key_grad = jnp.einsum("mhqk,mhqd->mhkd", score_low, query_rows, preferred_element_type=f32)
    pair_grad = jnp.stack([key_grad, value_grad])
    arrived = swap(pair_grad[..., rows:, :].astype(bf16), "ctx", 1)
    arrived = tie(arrived, expert_down_grad, shared_down_grad, my_out)
    gate_last = sum_ctx_parts(tie(gate_whole[:, cut_at:], arrived))
    up_piece = sum_ctx_parts(tie(up_whole, arrived))
    key_grad, value_grad = pair_grad[..., :rows, :] + arrived.astype(f32)
    proj_grad = jnp.concatenate(
        [
            flat(rotate(query_grad * score_scale, cosine, -sine_table).astype(bf16)),
            flat(rotate(key_grad * score_scale, cosine, -sine_table).astype(bf16)),
            flat(value_grad.astype(bf16)),
        ],
        axis=1,
    )
    one_terms = dot_cols(proj_grad, qkv_full)
    qkv_grad = dot_rows(normed_one, proj_grad).astype(bf16)
    qkv_summed = sum_shard(qkv_grad.reshape(n_sh, n_ctx * own, -1))
    qkv_grad = sum_ctx(qkv_summed.reshape(n_ctx, own, -1))
    turned_gate, shared_gate_grad = settle(
        tie(jnp.concatenate([gate_first, gate_last]), qkv_summed)
    )
    expert_gate_grad, shared_gate_grad = turned_gate.transpose(0, 2, 1), shared_gate_grad.T
    qkv_grad = qkv_grad.reshape(own, 3, heads_width).transpose(1, 0, 2)
    count = n_sh * n_ctx
    bias_own = head_dim // count
    bias_grad = jnp.sum(proj_grad.astype(f32), axis=0)
    bias_grad = bias_grad.reshape(3 * local_heads, head_dim)
    wide = inputs.astype(f32)
    factor = lax.rsqrt(jnp.mean(wide * wide, axis=-1, keepdims=True) + epsilon)
    attn_gain_grad = jnp.sum(one_terms * (wide * factor), axis=0, keepdims=True)
    late = jnp.concatenate([routing_grad, ffn_gain_grad[None], attn_gain_grad], axis=0)
    late = jnp.concatenate(
        [
            late.reshape(-1, count, own).transpose(1, 0, 2).reshape(count, -1),
            bias_grad.reshape(-1, count, bias_own).transpose(1, 0, 2).reshape(count, -1),
        ],
        axis=1,
    )
    late = jnp.sum(lax.all_to_all(late, ("shard", "ctx"), 0, 0, tiled=True), axis=0)
    bias_grad = late[(experts + 3) * own :].reshape(3, local_heads, bias_own)
    late = sum_tp_small(late[: (experts + 3) * own]).reshape(experts + 3, own)
    turned_up, shared_up_grad = settle(tie(up_piece, turned_gate))
    expert_up_grad, shared_up_grad = turned_up.transpose(0, 2, 1), shared_up_grad.T
    normed_one_grad = sum_tp(one_terms.reshape(n_tp, part, width))
    _, first_pull = jax.vjp(lambda v: rms_scale(v, first_gain), my_inputs)
    (input_norm_grad,) = first_pull(normed_one_grad)
    my_tokens_grad = (hidden_grad + input_norm_grad).astype(bf16)
    my_tokens_grad = tie(my_tokens_grad, turned_gate)
    tokens_grad = gather_tp(my_tokens_grad).astype(f32)

    layer_out = gather_tp(my_out)
    shape = (micro, 1, rows, width)
    return (
        layer_out.reshape(shape),
        tokens_grad.reshape(shape),
        late[experts + 2],
        qkv_grad,
        bias_grad,
        out_weight_grad,
        late[experts + 1],
        late[:experts].T,
        expert_gate_grad,
        expert_up_grad,
        expert_down_grad,
        shared_gate_grad,
        shared_up_grad,
        shared_down_grad,
        late[experts],
    )


def solution(mesh):
    in_specs = (
        P(None, "shard", "ctx", None),
        P(None, "shard", "ctx", None),
        P(None, "shard", "ctx", None),
        P(None, "shard"),
        P("shard"),
        P(None, "shard", "tp"),
        P(None, "tp", None),
        P("tp", "shard"),
        P("shard"),
        P("shard", None),
        P(None, "shard", "tp"),
        P(None, "shard", "tp"),
        P(None, "tp", "shard"),
        P("shard", "tp"),
        P("shard", "tp"),
        P("tp", "shard"),
        P("shard"),
    )
    out_specs = (
        P(None, "shard", "ctx", None),
        P(None, "shard", "ctx", None),
        P(("shard", "ctx")),
        P(None, ("shard", "ctx"), "tp"),
        P(None, "tp", ("shard", "ctx")),
        P("tp", ("shard", "ctx")),
        P(("shard", "ctx")),
        P(("shard", "ctx"), None),
        P(None, ("shard", "ctx"), "tp"),
        P(None, ("shard", "ctx"), "tp"),
        P(None, "tp", ("shard", "ctx")),
        P(("shard", "ctx"), "tp"),
        P(("shard", "ctx"), "tp"),
        P("tp", ("shard", "ctx")),
        P(("shard", "ctx")),
    )
    return jax.shard_map(body, mesh=mesh, in_specs=in_specs, out_specs=out_specs, check_vma=False)
```

```python
import functools

import jax
import jax.numpy as jnp
import numpy as np
from jax import lax
from jax.experimental import pallas as pl
from jax.experimental.pallas import tpu as pltpu
from jax.sharding import PartitionSpec as P

epsilon = 1e-06
rope_base = 1000000.0
highest = lax.Precision.HIGHEST
f32 = jnp.float32
bf16 = jnp.bfloat16
small_cost = pl.CostEstimate(flops=1000, bytes_accessed=1000, transcendentals=0)


def rms_scale(values, gain_vec):
    factor = lax.rsqrt(jnp.mean(values * values, axis=-1, keepdims=True) + epsilon)
    return values * factor * gain_vec


def rope_tables(length, head_dim):
    half_dim = head_dim // 2
    frequency = rope_base ** (-(np.arange(half_dim) * 2.0) / head_dim)
    places = np.arange(length)[:, None] * frequency[None, :]
    return jnp.asarray(np.cos(places), f32), jnp.asarray(np.sin(places), f32)


def rotate(values, cosine, sine_table):
    half_dim = values.shape[-1] // 2
    first_half = values[..., :half_dim]
    second_half = values[..., half_dim:]
    return jnp.concatenate(
        [
            first_half * cosine - second_half * sine_table,
            second_half * cosine + first_half * sine_table,
        ],
        axis=-1,
    )


def dot(left, right):
    return jnp.dot(left, right, preferred_element_type=f32)


def dot_rows(left, right):
    return lax.dot_general(left, right, (((0,), (0,)), ((), ())), preferred_element_type=f32)


def dot_cols(left, right):
    return lax.dot_general(left, right, (((1,), (1,)), ((), ())), preferred_element_type=f32)


def swap(values, axis, bit):
    count = lax.axis_size(axis)
    return lax.ppermute(values, axis, [(i, i ^ bit) for i in range(count)])


def pick(values, place, axis):
    return lax.dynamic_index_in_dim(values, place, axis, keepdims=False)


def sum_tp(terms):
    count = lax.axis_size("tp")
    place = lax.axis_index("tp")
    bit = 1
    while bit < count:
        pairs = terms.reshape((terms.shape[0] // 2, 2) + terms.shape[1:])
        low = (place // bit) % 2
        sent = pick(pairs, 1 - low, 1).astype(bf16)
        terms = pick(pairs, low, 1).astype(f32) + swap(sent, "tp", bit).astype(f32)
        bit *= 2
    return terms[0]


def gather_tp(block):
    count = lax.axis_size("tp")
    place = lax.axis_index("tp")
    held = block[None]
    bit = count // 2
    while bit >= 1:
        other = swap(held, "tp", bit)
        high = (place // bit) % 2
        held = jnp.where(
            high == 0, jnp.stack([held, other], 1), jnp.stack([other, held], 1)
        ).reshape((held.shape[0] * 2,) + block.shape)
        bit //= 2
    return held.reshape((count * block.shape[0],) + block.shape[1:])


def round_up(size):
    return -(-size // 128) * 128


def pad_to(values, axis, size):
    room = [(0, 0)] * values.ndim
    room[axis] = (0, size - values.shape[axis])
    return jnp.pad(values, room)


def tie(values, *after):
    return lax.optimization_barrier((values,) + after)[0]


def core_groups():
    n_sh, half = lax.axis_size("shard"), lax.axis_size("tp") // 2
    return [
        [s * 2 * half + z * 2 + core for s in range(n_sh) for z in range(half)]
        for core in range(2)
    ]


def exchange(values):
    return lax.all_to_all(
        values, ("shard", "tp"), 0, 0, tiled=True, axis_index_groups=core_groups()
    )


def gather_core(block):
    peers = lax.axis_size("shard") * lax.axis_size("tp") // 2
    return exchange(jnp.broadcast_to(block[None], (peers,) + block.shape))


def both_cores(own):
    flat = (own.shape[0] * own.shape[1], own.shape[2])
    return own.reshape(flat), swap(own, "tp", 1).reshape(flat)


def sum_shard(pieces):
    z = lax.axis_index("tp") // 2
    own = sum(piece.astype(f32) for piece in pieces)
    return pick(own, z, 0), pick(own, 1 - z, 0).astype(bf16)


def swap_z(sent):
    return swap(sent, "tp", 2).astype(f32)


def sum_tp_small(terms):
    bit = 1
    while bit < lax.axis_size("tp"):
        terms = terms + swap(terms, "tp", bit)
        bit *= 2
    return terms


def others(values, axis):
    count = lax.axis_size(axis)
    return [values[0]] + [swap(values[k], axis, k) for k in range(1, count)]


def in_order(pieces, axis):
    place = lax.axis_index(axis) ^ jnp.arange(len(pieces), dtype=jnp.int32)
    return jnp.take(jnp.stack(pieces), place, axis=0)


def place_kernel(count, place, rows, *refs):
    out = refs[-1]
    size = rows.shape[0] // count
    room = round_up(size)
    for k in range(count):
        part = rows[k * size : (k + 1) * size]
        if room > size:
            part = jnp.concatenate(
                [part, jnp.zeros((room - size, part.shape[1]), part.dtype)], axis=0
            )
        out[k * room : (k + 1) * room, :] = part


def place_columns(values, count, held, place, parts):
    rows, depth = values.shape
    n_sh = lax.axis_size("shard")
    chunk = depth // parts
    height = count * round_up(rows // count)
    operands = [values]
    specs = [pl.BlockSpec((rows, chunk), lambda c, at: (0, c))]
    aliases = {}
    if held is not None:
        aliases = {2: 0}
        operands.append(held)
        specs.append(pl.BlockSpec(memory_space=pl.ANY))
    return pl.pallas_call(
        functools.partial(place_kernel, count),
        grid_spec=pltpu.PrefetchScalarGridSpec(
            num_scalar_prefetch=1,
            grid=(parts,),
            in_specs=specs,
            out_specs=pl.BlockSpec((height, chunk), lambda c, at: (0, c * n_sh + at[0])),
        ),
        out_shape=jax.ShapeDtypeStruct((height, n_sh * depth), bf16),
        input_output_aliases=aliases,
        compiler_params=pltpu.CompilerParams(vmem_limit_bytes=32 * 2**20),
        cost_estimate=pl.CostEstimate(
            flops=0, bytes_accessed=4 * height * depth, transcendentals=0
        ),
    )(jnp.reshape(place, (1,)), *operands)


def hidden_kernel(
    bounds, step, values_a, values_b, up_a, up_b, gate_up, down, gates, act_out, grad_out, terms_out
):
    block = down.shape[0]
    pairs = pl.num_programs(0) // 2
    first = pl.program_id(0) < pairs
    values = jnp.where(first, values_a[...], values_b[...])
    up = jnp.where(first, up_a[...], up_b[...])
    tile = values.shape[0]
    count = len(bounds)
    gate_columns = [gates[:, k : k + 1] for k in range(count)]
    named_columns = [gates[:, count + k : count + k + 1] for k in range(count)]
    lane = lax.broadcasted_iota(jnp.int32, (1, 128), 1)
    terms = jnp.zeros((tile, 128), f32)
    for j in range(block // step):
        at = j * step
        pre_gate = dot_cols(values, gate_up[at : at + step, :])
        pre_up = dot_cols(values, gate_up[block + at : block + at + step, :])
        back = dot_cols(up, down[at : at + step, :])
        column = at + lax.broadcasted_iota(jnp.int32, (1, step), 1)
        sigma = jax.nn.sigmoid(pre_gate)
        silu = pre_gate * sigma
        act = silu * pre_up
        product = act * back
        wide = jnp.zeros((tile, step), f32)
        low = 0
        for k in range(count):
            if low < at + step and bounds[k] > at:
                inside = (column >= low) & (column < bounds[k])
                wide = jnp.where(inside, gate_columns[k], wide)
                term = jnp.sum(jnp.where(inside, product, 0.0), axis=1, keepdims=True)
                terms = terms + jnp.where(lane == k, term * named_columns[k], 0.0)
            low = bounds[k]
        act_grad = wide * back
        act_out[:, at : at + step] = (wide * act).astype(bf16)
        grad_out[:, at : at + step] = (act_grad * pre_up * (sigma + silu * (1.0 - sigma))).astype(
            bf16
        )
        grad_out[:, block + at : block + at + step] = (act_grad * silu).astype(bf16)
    terms_out[...] = terms


def hidden_units(values, up, gate_up, down, gates, bounds):
    half, width = values[0].shape
    block = down.shape[0]
    tile = half // 2 if half % 32 == 0 and half <= 1024 else 384
    pairs = half // tile
    own_rows = pl.BlockSpec((tile, width), lambda i: (jnp.minimum(i, pairs - 1), 0))
    other_rows = pl.BlockSpec((tile, width), lambda i: (jnp.maximum(i - pairs, 0), 0))
    return pl.pallas_call(
        functools.partial(hidden_kernel, bounds, 128 if block % 384 else 384),
        grid=(2 * pairs,),
        in_specs=[
            own_rows,
            other_rows,
            own_rows,
            other_rows,
            pl.BlockSpec((2 * block, width), lambda i: (0, 0), pipeline_mode=pl.Buffered(1)),
            pl.BlockSpec((block, width), lambda i: (0, 0), pipeline_mode=pl.Buffered(1)),
            pl.BlockSpec((tile, 128), lambda i: (i, 0)),
        ],
        out_specs=[
            pl.BlockSpec((tile, block), lambda i: (i, 0)),
            pl.BlockSpec((tile, 2 * block), lambda i: (i, 0)),
            pl.BlockSpec((tile, 128), lambda i: (i, 0)),
        ],
        out_shape=[
            jax.ShapeDtypeStruct((2 * half, block), bf16),
            jax.ShapeDtypeStruct((2 * half, 2 * block), bf16),
            jax.ShapeDtypeStruct((2 * half, 128), f32),
        ],
        compiler_params=pltpu.CompilerParams(vmem_limit_bytes=60 * 2**20),
        cost_estimate=small_cost,
    )(values[0], values[1], up[0], up[1], gate_up, down, gates)


def rows_kernel(left, right, *refs):
    out = refs[-1]
    value = dot(left[...], right[...])
    if len(refs) > 1:
        value = value + refs[0][...].astype(f32)
    out[...] = value.astype(bf16)


def cost(flops, nbytes):
    return pl.CostEstimate(flops=flops, bytes_accessed=nbytes, transcendentals=0)


def rows_dot(left, which, right, add=None, urgent=True):
    half, depth = left.shape[0] // 2, left.shape[1]
    width = right.shape[1]
    step = 512
    specs = [
        pl.BlockSpec((half, depth), lambda j: (which, 0), pipeline_mode=pl.Buffered(1)),
        pl.BlockSpec((depth, step), lambda j: (0, j)),
    ]
    out_spec = pl.BlockSpec((half, step), lambda j: (0, j))
    operands = [left, right]
    if add is not None:
        operands.append(add)
        specs.append(out_spec)
    return pl.pallas_call(
        rows_kernel,
        grid=(width // step,),
        in_specs=specs,
        out_specs=out_spec,
        out_shape=jax.ShapeDtypeStruct((half, width), bf16),
        compiler_params=pltpu.CompilerParams(vmem_limit_bytes=56 * 2**20),
        cost_estimate=small_cost if urgent else cost(2 * half * depth * width, 8 * half * width),
    )(*operands)


def units_kernel(used, units, values_a, values_b, out, turned):
    half = values_a.shape[0]

    @pl.when(pl.program_id(0) == 0)
    def _():
        for j in range(units.shape[0] // 128):
            turned[:, j * 128 : (j + 1) * 128] = units[j * 128 : (j + 1) * 128, :].T

    value = dot(turned[:, :half], values_a[...]) + dot(turned[:, half:], values_b[...])
    out[0] = value[:used].astype(bf16)


def units_dot(units, which, used, values, parts):
    half, width = values[0].shape
    block = round_up(used)
    step = 256
    each = width // parts // step
    return pl.pallas_call(
        functools.partial(units_kernel, used),
        grid=(width // step,),
        in_specs=[
            pl.BlockSpec((2 * half, block), lambda j: (0, which), pipeline_mode=pl.Buffered(1)),
            pl.BlockSpec((half, step), lambda j: (0, j)),
            pl.BlockSpec((half, step), lambda j: (0, j)),
        ],
        out_specs=pl.BlockSpec((1, used, step), lambda j: (j // each, 0, j % each)),
        out_shape=jax.ShapeDtypeStruct((parts, used, width // parts), bf16),
        scratch_shapes=[pltpu.VMEM((block, 2 * half), bf16)],
        compiler_params=pltpu.CompilerParams(vmem_limit_bytes=56 * 2**20),
        cost_estimate=small_cost,
    )(units, values[0], values[1])


def unpack_kernel(place, *refs):
    count = len(refs) - 2
    one, two = refs[count:]
    first = one.shape[1]
    for step in range(count):

        @pl.when(pl.program_id(0) == step)
        def _(grads=refs[step]):
            one[0] = grads[:first].astype(f32)
            two[0] = grads[first:].astype(f32)


def unpack(pieces, place, first):
    count = len(pieces)
    units, own = pieces[0].shape

    def where(step, at):
        return (at[0] ^ step, 0, 0)

    return pl.pallas_call(
        unpack_kernel,
        grid_spec=pltpu.PrefetchScalarGridSpec(
            num_scalar_prefetch=1,
            grid=(count,),
            in_specs=[pl.BlockSpec((units, own), lambda step, at: (0, 0))] * count,
            out_specs=[
                pl.BlockSpec((1, first, own), where),
                pl.BlockSpec((1, units - first, own), where),
            ],
        ),
        out_shape=[
            jax.ShapeDtypeStruct((count, first, own), f32),
            jax.ShapeDtypeStruct((count, units - first, own), f32),
        ],
        compiler_params=pltpu.CompilerParams(vmem_limit_bytes=32 * 2**20),
        cost_estimate=pl.CostEstimate(
            flops=0, bytes_accessed=6 * count * own * units, transcendentals=0
        ),
    )(jnp.reshape(place, (1,)), *pieces)


def body(
    tokens_in,
    cotangent,
    expert_ids,
    prefix_len,
    attn_gain,
    qkv_weight,
    qkv_bias,
    out_weight,
    ffn_gain,
    router_weight,
    expert_gate,
    expert_up,
    expert_down,
    shared_gate,
    shared_up,
    shared_down,
    shared_switch,
):
    n_sh, n_ctx, n_tp = lax.axis_size("shard"), lax.axis_size("ctx"), lax.axis_size("tp")
    my_sh, my_ctx, my_tp = lax.axis_index("shard"), lax.axis_index("ctx"), lax.axis_index("tp")
    micro, _, rows, width = tokens_in.shape
    picks = expert_ids.shape[-1]
    tok = micro * rows
    part = tok // n_tp
    total = n_sh * tok
    length = rows * n_ctx
    depth = qkv_weight.shape[1]
    own = width // (n_sh * n_ctx)
    local_heads, head_dim = qkv_bias.shape[1:]
    heads_width = local_heads * head_dim
    experts, _, hidden = expert_gate.shape
    shared_hidden = shared_gate.shape[1]
    score_scale = head_dim ** (-0.5)
    per = max(experts // n_sh, 1)
    mine_first = experts * hidden // n_sh
    unit = mine_first // per
    used = mine_first + shared_hidden // n_sh
    block = round_up(used)

    inputs = tokens_in.reshape(tok, width)
    upstream = cotangent.reshape(tok, width)
    ids = expert_ids.reshape(tok, picks)

    def mine(values):
        return lax.dynamic_slice_in_dim(values, my_tp * part, part, 0)

    small = jnp.concatenate(
        [
            attn_gain,
            ffn_gain,
            shared_switch,
            router_weight.T.reshape(-1),
            ids.astype(bf16).reshape(-1),
        ]
    )
    small = in_order(others([small] * n_sh, "shard"), "shard")
    first_gain = small[:, :depth].reshape(width).astype(f32)
    second_gain = small[:, depth : 2 * depth].reshape(width).astype(f32)
    switch_vec = small[:, 2 * depth : 3 * depth].reshape(width)
    router_full = (
        small[:, 3 * depth : (3 + experts) * depth]
        .reshape(n_sh, experts, depth)
        .transpose(0, 2, 1)
        .reshape(width, experts)
    )
    ids_all = small[:, (3 + experts) * depth :].reshape(n_sh * n_tp // 2, 2, part, picks)
    core = my_tp % 2
    ids_all = jnp.stack([pick(ids_all, core, 1), pick(ids_all, 1 - core, 1)])
    ids_all = ids_all.reshape(total, picks).astype(jnp.int32)

    qkv_local = qkv_weight.transpose(1, 0, 2).reshape(depth, 3 * heads_width)
    qkv_full = lax.all_gather(qkv_local, "shard", axis=0, tiled=True)
    bias_row = qkv_bias.reshape(1, 3 * heads_width).astype(f32)
    out_full = lax.all_gather(out_weight, "shard", axis=1, tiled=True)

    parts = n_ctx if own % 128 == 0 else 1
    chunk = depth // parts

    def to_parts(values):
        shape = values.shape[:-1]
        values = values.reshape(shape + (n_sh, parts, chunk))
        return values.swapaxes(-3, -2).reshape(shape + (width,))

    def from_parts(values):
        shape = values.shape[:-1]
        values = values.reshape(shape + (parts, n_sh, chunk))
        return values.swapaxes(-3, -2).reshape(shape + (width,))

    gate_up_local = (
        expert_gate.transpose(0, 2, 1).reshape(n_sh, mine_first, depth),
        shared_gate.T.reshape(n_sh, used - mine_first, depth),
        expert_up.transpose(0, 2, 1).reshape(n_sh, mine_first, depth),
        shared_up.T.reshape(n_sh, used - mine_first, depth),
    )
    down_local = (
        expert_down.reshape(n_sh, mine_first, depth),
        shared_down.reshape(n_sh, used - mine_first, depth),
    )

    def fetch(values, k, after):
        values = jnp.concatenate([pick(v, my_sh ^ k, 0) for v in values])
        return swap(tie(values, after), "shard", k) if k else values

    def fetch_gate_up(which, after, held):
        for k in which:
            values = fetch(gate_up_local, k, after)
            held = place_columns(values, 2, held, my_sh ^ k, parts)
        return held

    near, far = range(n_sh // 2 + 1), range(n_sh // 2 + 1, n_sh)

    normed_one = rms_scale(inputs.astype(f32), first_gain).astype(bf16)
    projected = (dot(normed_one, qkv_full) + bias_row).astype(bf16)

    def heads(values):
        return values.reshape(micro, rows, local_heads, head_dim).transpose(0, 2, 1, 3)

    def flat(values):
        return values.transpose(0, 2, 1, 3).reshape(tok, heads_width)

    cosine, sine_table = rope_tables(length, head_dim)
    cosine = lax.dynamic_slice_in_dim(cosine, my_ctx * rows, rows, 0)
    sine_table = lax.dynamic_slice_in_dim(sine_table, my_ctx * rows, rows, 0)
    query_rows, key_rows = (
        rotate(
            heads(projected[:, k * heads_width : (k + 1) * heads_width]).astype(f32),
            cosine,
            sine_table,
        ).astype(bf16)
        for k in range(2)
    )
    value_rows = heads(projected[:, 2 * heads_width :])
    own_rows = jnp.stack([key_rows, value_rows])
    other_rows = swap(own_rows, "ctx", 1)
    gate_up = fetch_gate_up(near, qkv_full, None)
    key_all, value_all = jnp.concatenate([own_rows, other_rows], axis=3)
    steps = jnp.arange(rows, dtype=jnp.int32)
    query_at = my_ctx * rows + steps
    key_at = jnp.concatenate([query_at, (1 - my_ctx) * rows + steps])
    allowed = (key_at[None, :] <= query_at[:, None])[None] | (
        key_at[None, None, :] < prefix_len.reshape(micro, 1, 1)
    )
    scores = (
        jnp.einsum("mhqd,mhkd->mhqk", query_rows, key_all, preferred_element_type=f32)
        * score_scale
    )
    scores = jnp.where(allowed[:, None], scores, -1000000000.0)
    raised = jnp.exp(scores - jnp.max(scores, axis=-1, keepdims=True))
    probs = raised / jnp.sum(raised, axis=-1, keepdims=True)
    probs_low = probs.astype(bf16)
    head_rows = flat(
        jnp.einsum("mhqk,mhkd->mhqd", probs_low, value_all, preferred_element_type=f32).astype(
            bf16
        )
    )
    head_rows = tie(head_rows, gate_up)
    gate_up = fetch_gate_up(far, other_rows, gate_up)
    down_pieces = [fetch(down_local, k, head_rows) for k in range(n_sh)]
    up_spread = to_parts(mine(upstream))
    up_spread = jnp.broadcast_to(up_spread[None], (n_sh * n_tp // 2, part, width))
    attn_total = sum_tp(dot(head_rows, out_full).reshape(n_tp, part, width))

    my_inputs = mine(inputs).astype(f32)
    my_up = mine(upstream).astype(f32)
    hidden_res = my_inputs + tie(attn_total, gate_up, up_spread, *down_pieces)
    second_float, second_pull = jax.vjp(rms_scale, hidden_res, second_gain)
    my_normed = second_float.astype(bf16)
    normed_core = gather_core(to_parts(my_normed))
    normed_two = both_cores(normed_core)
    up_core = exchange(tie(up_spread, normed_core))
    routing = jnp.concatenate([router_full, switch_vec[:, None]], axis=1)

    def route(values, weights):
        logits = dot(values, weights)
        return jax.nn.softmax(logits[:, :experts], axis=-1), jax.nn.sigmoid(logits[:, experts])

    routing_parts = to_parts(routing.T).T
    probs_all, switch_all = (
        jnp.concatenate(both) for both in zip(*(route(v, routing_parts) for v in normed_two))
    )
    first_expert = my_sh * experts // n_sh
    gates, names, bounds = [], [], []
    for k in range(per):
        named = jnp.any(ids_all == first_expert + k, axis=1)
        chosen = lax.dynamic_index_in_dim(probs_all, first_expert + k, 1, keepdims=False)
        names.append(named.astype(f32))
        gates.append(jnp.where(named, chosen, 0.0))
        bounds.append((k + 1) * unit)
    gates.append(switch_all)
    names.append(jnp.ones_like(switch_all))
    bounds.append(used)
    gates = pad_to(jnp.stack(gates + names, axis=1), 1, 128)

    up_all = both_cores(up_core)
    down = None
    for k in range(n_sh):
        down = place_columns(down_pieces[k], 1, down, my_sh ^ k, parts)
    act_low, pre_grad, gate_terms = hidden_units(
        normed_two, up_all, gate_up, down, gates, tuple(bounds)
    )
    lane = lax.broadcasted_iota(jnp.int32, (1, 128), 1)
    gate_terms = sum(
        jnp.where(lane == (first_expert + k if k < per else experts), gate_terms[:, k : k + 1], 0.0)
        for k in range(per + 1)
    )
    half = total // 2
    peers = n_sh * n_tp // 2

    def grad_whole(units, which, values):
        whole = units_dot(units, which, used, values, parts)
        if parts == n_ctx:
            return whole
        whole = whole.reshape(used, n_sh, n_ctx, own)
        return whole.transpose(2, 0, 1, 3).reshape(n_ctx, used, -1)

    def sum_ctx_parts(whole):
        return lax.psum_scatter(whole, "ctx", scatter_dimension=0, tiled=True)

    def sum_core(left, right, urgent):
        arrived = swap(rows_dot(left, 1, right, None, urgent), "tp", 1)
        return rows_dot(left, 0, right, arrived, urgent)

    def by_shard(own):
        own = own.reshape(n_sh, n_tp // 2, part, own.shape[-1])
        return [pick(own, my_sh ^ k, 0) for k in range(n_sh)]

    gate_terms = gate_terms.reshape(2, half, gate_terms.shape[-1])
    gate_terms = (gate_terms[0] + swap(gate_terms[1], "tp", 1)).astype(bf16)
    down_whole = grad_whole(act_low, 0, up_all)
    down_piece = sum_ctx_parts(down_whole)
    own_grad = sum_core(tie(pre_grad, down_whole), gate_up, True)
    own_grad = by_shard(jnp.concatenate([own_grad, gate_terms], axis=1))
    own_mixed = sum_core(tie(act_low, *own_grad), down, False)
    own_grad = [tie(v, own_mixed) for v in others(own_grad, "shard")]
    mixed = [tie(v, *own_grad) for v in by_shard(own_mixed)]
    mixed = others(mixed, "shard")
    grad_kept, grad_sent = sum_shard(own_grad)
    gate_whole = grad_whole(tie(pre_grad, grad_sent), 0, normed_two)
    gate_piece = sum_ctx_parts(gate_whole)
    normed_grad = grad_kept + tie(swap_z(grad_sent), gate_whole)
    gate_terms = normed_grad[:, width:]
    normed_grad = from_parts(normed_grad[:, :width])

    def owned(piece):
        return [
            lax.dynamic_slice_in_dim(piece[0], (my_sh ^ k) * own, own, 1) for k in range(n_sh)
        ]

    def settle(pieces, *after):
        return unpack([tie(p, *after) for p in pieces], my_sh, mine_first)

    def turned(one, two):
        one = one.reshape(experts, hidden, own).transpose(0, 2, 1)
        return one, two.reshape(shared_hidden, own).T

    my_probs, my_switch = route(my_normed, routing)
    prob_grads = gate_terms[:, :experts]
    logit_grads = my_probs * (
        prob_grads - jnp.sum(my_probs * prob_grads, axis=-1, keepdims=True)
    )
    switch_pre_grad = gate_terms[:, experts] * my_switch * (1.0 - my_switch)
    route_grads = jnp.concatenate([logit_grads, switch_pre_grad[:, None]], axis=1)
    normed_float = my_normed.astype(f32)
    routing_grad = lax.dot_general(
        route_grads, normed_float, (((0,), (0,)), ((), ())), precision=highest
    )
    normed_grad = normed_grad + lax.dot_general(
        route_grads, routing.astype(f32), (((1,), (1,)), ((), ())), precision=highest
    )
    hidden_norm_grad, ffn_gain_grad = second_pull(normed_grad)
    hidden_grad = my_up + hidden_norm_grad

    def pieces_of(terms):
        return [pick(terms, my_sh ^ k, 0) for k in range(n_sh)]

    def sum_pieces(pieces, *after):
        return sum(tie(piece, *after).astype(f32) for piece in others(pieces, "shard"))

    def for_other(terms):
        return pick(terms, 1 - my_ctx, 0).astype(bf16)


    my_branch = hidden_grad.astype(bf16)
    up_whole = grad_whole(tie(pre_grad, my_branch), 1, normed_two)
    up_piece = sum_ctx_parts(up_whole)
    down_terms = others(owned(down_piece), "shard")
    mixed_kept, mixed_sent = sum_shard([tie(v, my_branch) for v in mixed])
    branch_low = tie(gather_tp(my_branch), up_whole, mixed_sent, *down_terms)
    out_weight_grad = dot_rows(head_rows, branch_low).astype(bf16)
    out_terms = [
        lax.dynamic_slice_in_dim(out_weight_grad, (my_sh ^ k) * n_ctx * own, n_ctx * own, 1)
        for k in range(n_sh)
    ]
    head_grad = dot_cols(branch_low, out_full).astype(bf16)
    head_grad = heads(head_grad)
    prob_grad = jnp.einsum("mhqd,mhkd->mhqk", head_grad, value_all, preferred_element_type=f32)
    value_grad = jnp.einsum("mhqk,mhqd->mhkd", probs_low, head_grad, preferred_element_type=f32)
    score_low = (
        probs * (prob_grad - jnp.sum(probs * prob_grad, axis=-1, keepdims=True))
    ).astype(bf16)
    query_grad = jnp.einsum("mhqk,mhkd->mhqd", score_low, key_all, preferred_element_type=f32)
    key_grad = jnp.einsum("mhqk,mhqd->mhkd", score_low, query_rows, preferred_element_type=f32)
    pair_grad = jnp.stack([key_grad, value_grad])
    pair_sent = pair_grad[..., rows:, :].astype(bf16)
    arrived = swap(pair_sent, "ctx", 1)
    down_parts = settle(down_terms, pair_sent)
    expert_down_grad = down_parts[0].reshape(experts, hidden, own)
    shared_down_grad = down_parts[1].reshape(shared_hidden, own)
    out_summed = sum_pieces(out_terms, pair_sent)
    gate_parts = settle(others(owned(gate_piece), "shard"), pair_sent)
    mixed_sum = mixed_kept + swap_z(tie(mixed_sent, pair_sent))
    my_out = (hidden_res + from_parts(mixed_sum)).astype(bf16)
    layer_out = gather_tp(my_out)
    arrived = tie(arrived, my_out, *down_parts, out_summed, *gate_parts)
    key_grad, value_grad = pair_grad[..., :rows, :] + arrived.astype(f32)
    proj_grad = jnp.concatenate(
        [
            flat(rotate(query_grad * score_scale, cosine, -sine_table).astype(bf16)),
            flat(rotate(key_grad * score_scale, cosine, -sine_table).astype(bf16)),
            flat(value_grad.astype(bf16)),
        ],
        axis=1,
    )
    qkv_grad = dot_rows(normed_one, proj_grad).astype(bf16)
    qkv_terms = qkv_grad.reshape(n_sh, n_ctx * own, -1)
    in_square = n_sh == 4
    if in_square:
        my_x, my_y = my_sh % 2, my_sh // 2
        middle = qkv_terms.shape[2] // 2
        qkv_terms = qkv_terms.reshape(2, 2, n_ctx * own, -1)
        one_half, two_half = qkv_terms[..., :middle], qkv_terms[..., middle:]
        kept_terms = pick(one_half, my_x, 1), pick(two_half, my_y, 0)
        qkv_terms = [pick(one_half, 1 - my_x, 1), pick(two_half, 1 - my_y, 0)]
    else:
        qkv_terms = pieces_of(qkv_terms)
    one_terms = dot_cols(tie(proj_grad, *qkv_terms), qkv_full)
    count = n_sh * n_ctx
    bias_own = head_dim // count
    bias_grad = jnp.sum(proj_grad.astype(f32), axis=0)
    bias_grad = bias_grad.reshape(3 * local_heads, head_dim)
    wide = inputs.astype(f32)
    factor = lax.rsqrt(jnp.mean(wide * wide, axis=-1, keepdims=True) + epsilon)
    attn_gain_grad = jnp.sum(one_terms * (wide * factor), axis=0, keepdims=True)
    late = jnp.concatenate([routing_grad, ffn_gain_grad[None], attn_gain_grad], axis=0)
    late = jnp.concatenate(
        [
            late.reshape(-1, count, own).transpose(1, 0, 2).reshape(count, -1),
            bias_grad.reshape(-1, count, bias_own).transpose(1, 0, 2).reshape(count, -1),
        ],
        axis=1,
    )
    expert_gate_grad, shared_gate_grad = turned(*gate_parts)
    out_summed = tie(out_summed, one_terms).reshape(-1, n_ctx, own).transpose(1, 0, 2)
    out_got = swap(for_other(out_summed), "ctx", 1)
    out_weight_grad = pick(out_summed, my_ctx, 0) + out_got.astype(f32)
    normed_one_grad = sum_tp(one_terms.reshape(n_tp, part, width))
    if in_square:
        one_half = kept_terms[0].astype(f32) + swap(qkv_terms[0], "shard", 1).astype(f32)
        two_half = kept_terms[1].astype(f32) + swap(qkv_terms[1], "shard", 2).astype(f32)
        kept_terms = pick(one_half, my_y, 0), pick(two_half, my_x, 0)
        qkv_terms = [
            pick(one_half, 1 - my_y, 0).astype(bf16),
            pick(two_half, 1 - my_x, 0).astype(bf16),
        ]
        normed_one_grad = tie(normed_one_grad, *qkv_terms)
    _, first_pull = jax.vjp(lambda v: rms_scale(v, first_gain), my_inputs)
    (input_norm_grad,) = first_pull(normed_one_grad)
    my_tokens_grad = tie((hidden_grad + input_norm_grad).astype(bf16), out_got)
    tokens_grad = gather_tp(my_tokens_grad).astype(f32)
    late_rows = lax.all_to_all(tie(late, my_tokens_grad), ("shard", "ctx"), 0, 0, tiled=True)
    late = jnp.sum(late_rows, axis=0)
    bias_grad = late[(experts + 3) * own :].reshape(3, local_heads, bias_own)
    late = sum_tp_small(late[: (experts + 3) * own]).reshape(experts + 3, own)
    up_terms = owned(tie(up_piece, my_tokens_grad, late_rows))
    if in_square:
        qkv_got = [swap(qkv_terms[0], "shard", 2), swap(qkv_terms[1], "shard", 1)]
        qkv_summed = jnp.concatenate(
            [
                kept + tie(got, my_tokens_grad, *up_terms).astype(f32)
                for kept, got in zip(kept_terms, qkv_got)
            ],
            axis=1,
        )
    else:
        qkv_summed = sum_pieces(qkv_terms, my_tokens_grad, *up_terms)
    up_terms = others(up_terms, "shard")
    qkv_summed = qkv_summed.reshape(n_ctx, own, -1)
    qkv_sent = for_other(qkv_summed)
    qkv_got = swap(qkv_sent, "ctx", 1)
    qkv_grad = pick(qkv_summed, my_ctx, 0) + qkv_got.astype(f32)
    qkv_grad = qkv_grad.reshape(own, 3, heads_width).transpose(1, 0, 2)

    expert_up_grad, shared_up_grad = turned(*settle(up_terms, qkv_got))
    shape = (micro, 1, rows, width)
    return (
        layer_out.reshape(shape),
        tokens_grad.reshape(shape),
        late[experts + 2],
        qkv_grad,
        bias_grad,
        out_weight_grad,
        late[experts + 1],
        late[:experts].T,
        expert_gate_grad,
        expert_up_grad,
        expert_down_grad,
        shared_gate_grad,
        shared_up_grad,
        shared_down_grad,
        late[experts],
    )


def solution(mesh):
    in_specs = (
        P(None, "shard", "ctx", None),
        P(None, "shard", "ctx", None),
        P(None, "shard", "ctx", None),
        P(None, "shard"),
        P("shard"),
        P(None, "shard", "tp"),
        P(None, "tp", None),
        P("tp", "shard"),
        P("shard"),
        P("shard", None),
        P(None, "shard", "tp"),
        P(None, "shard", "tp"),
        P(None, "tp", "shard"),
        P("shard", "tp"),
        P("shard", "tp"),
        P("tp", "shard"),
        P("shard"),
    )
    out_specs = (
        P(None, "shard", "ctx", None),
        P(None, "shard", "ctx", None),
        P(("shard", "ctx")),
        P(None, ("shard", "ctx"), "tp"),
        P(None, "tp", ("shard", "ctx")),
        P("tp", ("shard", "ctx")),
        P(("shard", "ctx")),
        P(("shard", "ctx"), None),
        P(None, ("shard", "ctx"), "tp"),
        P(None, ("shard", "ctx"), "tp"),
        P(None, "tp", ("shard", "ctx")),
        P(("shard", "ctx"), "tp"),
        P(("shard", "ctx"), "tp"),
        P("tp", ("shard", "ctx")),
        P(("shard", "ctx")),
    )
    return jax.shard_map(body, mesh=mesh, in_specs=in_specs, out_specs=out_specs, check_vma=False)
```

```python
import functools

import jax
import jax.numpy as jnp
import numpy as np
from jax import lax
from jax.experimental import pallas as pl
from jax.experimental.pallas import tpu as pltpu
from jax.sharding import PartitionSpec as P

epsilon = 1e-06
rope_base = 1000000.0
highest = lax.Precision.HIGHEST
f32 = jnp.float32
bf16 = jnp.bfloat16
small_cost = pl.CostEstimate(flops=1000, bytes_accessed=1000, transcendentals=0)


def rms_scale(values, gain_vec):
    factor = lax.rsqrt(jnp.mean(values * values, axis=-1, keepdims=True) + epsilon)
    return values * factor * gain_vec


def rope_tables(length, head_dim):
    half_dim = head_dim // 2
    frequency = rope_base ** (-(np.arange(half_dim) * 2.0) / head_dim)
    places = np.arange(length)[:, None] * frequency[None, :]
    return jnp.asarray(np.cos(places), f32), jnp.asarray(np.sin(places), f32)


def rotate(values, cosine, sine_table):
    half_dim = values.shape[-1] // 2
    first_half = values[..., :half_dim]
    second_half = values[..., half_dim:]
    return jnp.concatenate(
        [
            first_half * cosine - second_half * sine_table,
            second_half * cosine + first_half * sine_table,
        ],
        axis=-1,
    )


def dot(left, right):
    return jnp.dot(left, right, preferred_element_type=f32)


def dot_rows(left, right):
    return lax.dot_general(left, right, (((0,), (0,)), ((), ())), preferred_element_type=f32)


def dot_cols(left, right):
    return lax.dot_general(left, right, (((1,), (1,)), ((), ())), preferred_element_type=f32)


def swap(values, axis, bit):
    count = lax.axis_size(axis)
    return lax.ppermute(values, axis, [(i, i ^ bit) for i in range(count)])


def pick(values, place, axis):
    return lax.dynamic_index_in_dim(values, place, axis, keepdims=False)


def sum_tp(terms):
    count = lax.axis_size("tp")
    place = lax.axis_index("tp")
    bit = 1
    while bit < count:
        pairs = terms.reshape((terms.shape[0] // 2, 2) + terms.shape[1:])
        low = (place // bit) % 2
        sent = pick(pairs, 1 - low, 1).astype(bf16)
        terms = pick(pairs, low, 1).astype(f32) + swap(sent, "tp", bit).astype(f32)
        bit *= 2
    return terms[0]


def gather_tp(block):
    count = lax.axis_size("tp")
    place = lax.axis_index("tp")
    held = block[None]
    bit = count // 2
    while bit >= 1:
        other = swap(held, "tp", bit)
        high = (place // bit) % 2
        held = jnp.where(
            high == 0, jnp.stack([held, other], 1), jnp.stack([other, held], 1)
        ).reshape((held.shape[0] * 2,) + block.shape)
        bit //= 2
    return held.reshape((count * block.shape[0],) + block.shape[1:])


def round_up(size):
    return -(-size // 128) * 128


def pad_to(values, axis, size):
    room = [(0, 0)] * values.ndim
    room[axis] = (0, size - values.shape[axis])
    return jnp.pad(values, room)


def tie(values, *after):
    return lax.optimization_barrier((values,) + after)[0]


def core_groups():
    n_sh, half = lax.axis_size("shard"), lax.axis_size("tp") // 2
    return [
        [s * 2 * half + z * 2 + core for s in range(n_sh) for z in range(half)]
        for core in range(2)
    ]


def exchange(values):
    return lax.all_to_all(
        values, ("shard", "tp"), 0, 0, tiled=True, axis_index_groups=core_groups()
    )


def gather_core(block):
    peers = lax.axis_size("shard") * lax.axis_size("tp") // 2
    return exchange(jnp.broadcast_to(block[None], (peers,) + block.shape))


def both_cores(own):
    flat = (own.shape[0] * own.shape[1], own.shape[2])
    return own.reshape(flat), swap(own, "tp", 1).reshape(flat)


def sum_shard(pieces):
    z = lax.axis_index("tp") // 2
    own = sum(piece.astype(f32) for piece in pieces)
    return pick(own, z, 0), pick(own, 1 - z, 0).astype(bf16)


def swap_z(sent):
    return swap(sent, "tp", 2).astype(f32)


def sum_tp_small(terms):
    bit = 1
    while bit < lax.axis_size("tp"):
        terms = terms + swap(terms, "tp", bit)
        bit *= 2
    return terms


def others(values, axis):
    count = lax.axis_size(axis)
    return [values[0]] + [swap(values[k], axis, k) for k in range(1, count)]


def in_order(pieces, axis):
    place = lax.axis_index(axis) ^ jnp.arange(len(pieces), dtype=jnp.int32)
    return jnp.take(jnp.stack(pieces), place, axis=0)


def place_kernel(count, place, rows, *refs):
    out = refs[-1]
    size = rows.shape[0] // count
    room = round_up(size)
    for k in range(count):
        part = rows[k * size : (k + 1) * size]
        if room > size:
            part = jnp.concatenate(
                [part, jnp.zeros((room - size, part.shape[1]), part.dtype)], axis=0
            )
        out[k * room : (k + 1) * room, :] = part


def place_columns(values, count, held, place, parts):
    rows, depth = values.shape
    n_sh = lax.axis_size("shard")
    chunk = depth // parts
    height = count * round_up(rows // count)
    operands = [values]
    specs = [pl.BlockSpec((rows, chunk), lambda c, at: (0, c))]
    aliases = {}
    if held is not None:
        aliases = {2: 0}
        operands.append(held)
        specs.append(pl.BlockSpec(memory_space=pl.ANY))
    return pl.pallas_call(
        functools.partial(place_kernel, count),
        grid_spec=pltpu.PrefetchScalarGridSpec(
            num_scalar_prefetch=1,
            grid=(parts,),
            in_specs=specs,
            out_specs=pl.BlockSpec((height, chunk), lambda c, at: (0, c * n_sh + at[0])),
        ),
        out_shape=jax.ShapeDtypeStruct((height, n_sh * depth), bf16),
        input_output_aliases=aliases,
        compiler_params=pltpu.CompilerParams(vmem_limit_bytes=32 * 2**20),
        cost_estimate=pl.CostEstimate(
            flops=0, bytes_accessed=4 * height * depth, transcendentals=0
        ),
    )(jnp.reshape(place, (1,)), *operands)


def hidden_kernel(
    bounds, step, values_a, values_b, up_a, up_b, gate_up, down, gates, act_out, grad_out, terms_out
):
    block = down.shape[0]
    pairs = pl.num_programs(0) // 2
    first = pl.program_id(0) < pairs
    values = jnp.where(first, values_a[...], values_b[...])
    up = jnp.where(first, up_a[...], up_b[...])
    tile = values.shape[0]
    count = len(bounds)
    gate_columns = [gates[:, k : k + 1] for k in range(count)]
    named_columns = [gates[:, count + k : count + k + 1] for k in range(count)]
    lane = lax.broadcasted_iota(jnp.int32, (1, 128), 1)
    terms = jnp.zeros((tile, 128), f32)
    for j in range(block // step):
        at = j * step
        pre_gate = dot_cols(values, gate_up[at : at + step, :])
        pre_up = dot_cols(values, gate_up[block + at : block + at + step, :])
        back = dot_cols(up, down[at : at + step, :])
        column = at + lax.broadcasted_iota(jnp.int32, (1, step), 1)
        sigma = jax.nn.sigmoid(pre_gate)
        silu = pre_gate * sigma
        act = silu * pre_up
        product = act * back
        wide = jnp.zeros((tile, step), f32)
        low = 0
        for k in range(count):
            if low < at + step and bounds[k] > at:
                inside = (column >= low) & (column < bounds[k])
                wide = jnp.where(inside, gate_columns[k], wide)
                term = jnp.sum(jnp.where(inside, product, 0.0), axis=1, keepdims=True)
                terms = terms + jnp.where(lane == k, term * named_columns[k], 0.0)
            low = bounds[k]
        act_grad = wide * back
        act_out[:, at : at + step] = (wide * act).astype(bf16)
        grad_out[:, at : at + step] = (act_grad * pre_up * (sigma + silu * (1.0 - sigma))).astype(
            bf16
        )
        grad_out[:, block + at : block + at + step] = (act_grad * silu).astype(bf16)
    terms_out[...] = terms


def hidden_units(values, up, gate_up, down, gates, bounds):
    half, width = values[0].shape
    block = down.shape[0]
    tile = half // 2 if half % 32 == 0 and half <= 1024 else 384
    pairs = half // tile
    own_rows = pl.BlockSpec((tile, width), lambda i: (jnp.minimum(i, pairs - 1), 0))
    other_rows = pl.BlockSpec((tile, width), lambda i: (jnp.maximum(i - pairs, 0), 0))
    return pl.pallas_call(
        functools.partial(hidden_kernel, bounds, 128 if block % 384 else 384),
        grid=(2 * pairs,),
        in_specs=[
            own_rows,
            other_rows,
            own_rows,
            other_rows,
            pl.BlockSpec((2 * block, width), lambda i: (0, 0), pipeline_mode=pl.Buffered(1)),
            pl.BlockSpec((block, width), lambda i: (0, 0), pipeline_mode=pl.Buffered(1)),
            pl.BlockSpec((tile, 128), lambda i: (i, 0)),
        ],
        out_specs=[
            pl.BlockSpec((tile, block), lambda i: (i, 0)),
            pl.BlockSpec((tile, 2 * block), lambda i: (i, 0)),
            pl.BlockSpec((tile, 128), lambda i: (i, 0)),
        ],
        out_shape=[
            jax.ShapeDtypeStruct((2 * half, block), bf16),
            jax.ShapeDtypeStruct((2 * half, 2 * block), bf16),
            jax.ShapeDtypeStruct((2 * half, 128), f32),
        ],
        compiler_params=pltpu.CompilerParams(vmem_limit_bytes=60 * 2**20),
        cost_estimate=small_cost,
    )(values[0], values[1], up[0], up[1], gate_up, down, gates)


def rows_kernel(left, right, *refs):
    out = refs[-1]
    value = dot(left[...], right[...])
    if len(refs) > 1:
        value = value + refs[0][...].astype(f32)
    out[...] = value.astype(bf16)


def cost(flops, nbytes):
    return pl.CostEstimate(flops=flops, bytes_accessed=nbytes, transcendentals=0)


def rows_dot(left, which, right, add=None, urgent=True):
    half, depth = left.shape[0] // 2, left.shape[1]
    width = right.shape[1]
    step = 512
    specs = [
        pl.BlockSpec((half, depth), lambda j: (which, 0), pipeline_mode=pl.Buffered(1)),
        pl.BlockSpec((depth, step), lambda j: (0, j)),
    ]
    out_spec = pl.BlockSpec((half, step), lambda j: (0, j))
    operands = [left, right]
    if add is not None:
        operands.append(add)
        specs.append(out_spec)
    return pl.pallas_call(
        rows_kernel,
        grid=(width // step,),
        in_specs=specs,
        out_specs=out_spec,
        out_shape=jax.ShapeDtypeStruct((half, width), bf16),
        compiler_params=pltpu.CompilerParams(vmem_limit_bytes=56 * 2**20),
        cost_estimate=small_cost if urgent else cost(2 * half * depth * width, 8 * half * width),
    )(*operands)


def units_kernel(used, units, values_a, values_b, out, turned):
    half = values_a.shape[0]

    @pl.when(pl.program_id(0) == 0)
    def _():
        for j in range(units.shape[0] // 128):
            turned[:, j * 128 : (j + 1) * 128] = units[j * 128 : (j + 1) * 128, :].T

    value = dot(turned[:, :half], values_a[...]) + dot(turned[:, half:], values_b[...])
    out[0] = value[:used].astype(bf16)


def units_dot(units, which, used, values, parts):
    half, width = values[0].shape
    block = round_up(used)
    step = 256
    each = width // parts // step
    return pl.pallas_call(
        functools.partial(units_kernel, used),
        grid=(width // step,),
        in_specs=[
            pl.BlockSpec((2 * half, block), lambda j: (0, which), pipeline_mode=pl.Buffered(1)),
            pl.BlockSpec((half, step), lambda j: (0, j)),
            pl.BlockSpec((half, step), lambda j: (0, j)),
        ],
        out_specs=pl.BlockSpec((1, used, step), lambda j: (j // each, 0, j % each)),
        out_shape=jax.ShapeDtypeStruct((parts, used, width // parts), bf16),
        scratch_shapes=[pltpu.VMEM((block, 2 * half), bf16)],
        compiler_params=pltpu.CompilerParams(vmem_limit_bytes=56 * 2**20),
        cost_estimate=small_cost,
    )(units, values[0], values[1])


def unpack_kernel(place, *refs):
    count = len(refs) - 2
    one, two = refs[count:]
    first = one.shape[1]
    for step in range(count):

        @pl.when(pl.program_id(0) == step)
        def _(grads=refs[step]):
            one[0] = grads[:first].astype(f32)
            two[0] = grads[first:].astype(f32)


def unpack(pieces, place, first):
    count = len(pieces)
    units, own = pieces[0].shape

    def where(step, at):
        return (at[0] ^ step, 0, 0)

    return pl.pallas_call(
        unpack_kernel,
        grid_spec=pltpu.PrefetchScalarGridSpec(
            num_scalar_prefetch=1,
            grid=(count,),
            in_specs=[pl.BlockSpec((units, own), lambda step, at: (0, 0))] * count,
            out_specs=[
                pl.BlockSpec((1, first, own), where),
                pl.BlockSpec((1, units - first, own), where),
            ],
        ),
        out_shape=[
            jax.ShapeDtypeStruct((count, first, own), f32),
            jax.ShapeDtypeStruct((count, units - first, own), f32),
        ],
        compiler_params=pltpu.CompilerParams(vmem_limit_bytes=32 * 2**20),
        cost_estimate=pl.CostEstimate(
            flops=0, bytes_accessed=6 * count * own * units, transcendentals=0
        ),
    )(jnp.reshape(place, (1,)), *pieces)


def body(
    tokens_in,
    cotangent,
    expert_ids,
    prefix_len,
    attn_gain,
    qkv_weight,
    qkv_bias,
    out_weight,
    ffn_gain,
    router_weight,
    expert_gate,
    expert_up,
    expert_down,
    shared_gate,
    shared_up,
    shared_down,
    shared_switch,
):
    n_sh, n_ctx, n_tp = lax.axis_size("shard"), lax.axis_size("ctx"), lax.axis_size("tp")
    my_sh, my_ctx, my_tp = lax.axis_index("shard"), lax.axis_index("ctx"), lax.axis_index("tp")
    micro, _, rows, width = tokens_in.shape
    picks = expert_ids.shape[-1]
    tok = micro * rows
    part = tok // n_tp
    total = n_sh * tok
    length = rows * n_ctx
    depth = qkv_weight.shape[1]
    own = width // (n_sh * n_ctx)
    local_heads, head_dim = qkv_bias.shape[1:]
    heads_width = local_heads * head_dim
    experts, _, hidden = expert_gate.shape
    shared_hidden = shared_gate.shape[1]
    score_scale = head_dim ** (-0.5)
    per = max(experts // n_sh, 1)
    mine_first = experts * hidden // n_sh
    unit = mine_first // per
    used = mine_first + shared_hidden // n_sh
    block = round_up(used)

    inputs = tokens_in.reshape(tok, width)
    upstream = cotangent.reshape(tok, width)
    ids = expert_ids.reshape(tok, picks)

    def mine(values):
        return lax.dynamic_slice_in_dim(values, my_tp * part, part, 0)

    small = jnp.concatenate(
        [
            attn_gain,
            ffn_gain,
            shared_switch,
            router_weight.T.reshape(-1),
            ids.astype(bf16).reshape(-1),
        ]
    )
    small = in_order(others([small] * n_sh, "shard"), "shard")
    first_gain = small[:, :depth].reshape(width).astype(f32)
    second_gain = small[:, depth : 2 * depth].reshape(width).astype(f32)
    switch_vec = small[:, 2 * depth : 3 * depth].reshape(width)
    router_full = (
        small[:, 3 * depth : (3 + experts) * depth]
        .reshape(n_sh, experts, depth)
        .transpose(0, 2, 1)
        .reshape(width, experts)
    )
    ids_all = small[:, (3 + experts) * depth :].reshape(n_sh * n_tp // 2, 2, part, picks)
    core = my_tp % 2
    ids_all = jnp.stack([pick(ids_all, core, 1), pick(ids_all, 1 - core, 1)])
    ids_all = ids_all.reshape(total, picks).astype(jnp.int32)

    qkv_local = qkv_weight.transpose(1, 0, 2).reshape(depth, 3 * heads_width)
    qkv_full = lax.all_gather(qkv_local, "shard", axis=0, tiled=True)
    bias_row = qkv_bias.reshape(1, 3 * heads_width).astype(f32)
    out_full = lax.all_gather(out_weight, "shard", axis=1, tiled=True)

    parts = n_ctx if own % 128 == 0 else 1
    chunk = depth // parts

    def to_parts(values):
        shape = values.shape[:-1]
        values = values.reshape(shape + (n_sh, parts, chunk))
        return values.swapaxes(-3, -2).reshape(shape + (width,))

    def from_parts(values):
        shape = values.shape[:-1]
        values = values.reshape(shape + (parts, n_sh, chunk))
        return values.swapaxes(-3, -2).reshape(shape + (width,))

    gate_up_local = (
        expert_gate.transpose(0, 2, 1).reshape(n_sh, mine_first, depth),
        shared_gate.T.reshape(n_sh, used - mine_first, depth),
        expert_up.transpose(0, 2, 1).reshape(n_sh, mine_first, depth),
        shared_up.T.reshape(n_sh, used - mine_first, depth),
    )
    down_local = (
        expert_down.reshape(n_sh, mine_first, depth),
        shared_down.reshape(n_sh, used - mine_first, depth),
    )

    def fetch(values, k, after):
        values = jnp.concatenate([pick(v, my_sh ^ k, 0) for v in values])
        return swap(tie(values, after), "shard", k) if k else values

    def fetch_gate_up(which, after, held):
        for k in which:
            values = fetch(gate_up_local, k, after)
            held = place_columns(values, 2, held, my_sh ^ k, parts)
        return held

    near, far = range(n_sh // 2 + 1), range(n_sh // 2 + 1, n_sh)

    normed_one = rms_scale(inputs.astype(f32), first_gain).astype(bf16)
    projected = (dot(normed_one, qkv_full) + bias_row).astype(bf16)

    def heads(values):
        return values.reshape(micro, rows, local_heads, head_dim).transpose(0, 2, 1, 3)

    def flat(values):
        return values.transpose(0, 2, 1, 3).reshape(tok, heads_width)

    cosine, sine_table = rope_tables(length, head_dim)
    cosine = lax.dynamic_slice_in_dim(cosine, my_ctx * rows, rows, 0)
    sine_table = lax.dynamic_slice_in_dim(sine_table, my_ctx * rows, rows, 0)
    query_rows, key_rows = (
        rotate(
            heads(projected[:, k * heads_width : (k + 1) * heads_width]).astype(f32),
            cosine,
            sine_table,
        ).astype(bf16)
        for k in range(2)
    )
    value_rows = heads(projected[:, 2 * heads_width :])
    own_rows = jnp.stack([key_rows, value_rows])
    other_rows = swap(own_rows, "ctx", 1)
    gate_up = fetch_gate_up(near, qkv_full, None)
    key_all, value_all = jnp.concatenate([own_rows, other_rows], axis=3)
    steps = jnp.arange(rows, dtype=jnp.int32)
    query_at = my_ctx * rows + steps
    key_at = jnp.concatenate([query_at, (1 - my_ctx) * rows + steps])
    allowed = (key_at[None, :] <= query_at[:, None])[None] | (
        key_at[None, None, :] < prefix_len.reshape(micro, 1, 1)
    )
    scores = (
        jnp.einsum("mhqd,mhkd->mhqk", query_rows, key_all, preferred_element_type=f32)
        * score_scale
    )
    scores = jnp.where(allowed[:, None], scores, -1000000000.0)
    raised = jnp.exp(scores - jnp.max(scores, axis=-1, keepdims=True))
    probs = raised / jnp.sum(raised, axis=-1, keepdims=True)
    probs_low = probs.astype(bf16)
    head_rows = flat(
        jnp.einsum("mhqk,mhkd->mhqd", probs_low, value_all, preferred_element_type=f32).astype(
            bf16
        )
    )
    head_rows = tie(head_rows, gate_up)
    gate_up = fetch_gate_up(far, other_rows, gate_up)
    down_pieces = [fetch(down_local, k, head_rows) for k in range(n_sh)]
    up_spread = to_parts(mine(upstream))
    up_spread = jnp.broadcast_to(up_spread[None], (n_sh * n_tp // 2, part, width))
    attn_total = sum_tp(dot(head_rows, out_full).reshape(n_tp, part, width))

    my_inputs = mine(inputs).astype(f32)
    my_up = mine(upstream).astype(f32)
    hidden_res = my_inputs + tie(attn_total, gate_up, up_spread, *down_pieces)
    second_float, second_pull = jax.vjp(rms_scale, hidden_res, second_gain)
    my_normed = second_float.astype(bf16)
    normed_core = gather_core(to_parts(my_normed))
    normed_two = both_cores(normed_core)
    up_core = exchange(tie(up_spread, normed_core))
    routing = jnp.concatenate([router_full, switch_vec[:, None]], axis=1)

    def route(values, weights):
        logits = dot(values, weights)
        return jax.nn.softmax(logits[:, :experts], axis=-1), jax.nn.sigmoid(logits[:, experts])

    routing_parts = to_parts(routing.T).T
    probs_all, switch_all = (
        jnp.concatenate(both) for both in zip(*(route(v, routing_parts) for v in normed_two))
    )
    first_expert = my_sh * experts // n_sh
    gates, names, bounds = [], [], []
    for k in range(per):
        named = jnp.any(ids_all == first_expert + k, axis=1)
        chosen = lax.dynamic_index_in_dim(probs_all, first_expert + k, 1, keepdims=False)
        names.append(named.astype(f32))
        gates.append(jnp.where(named, chosen, 0.0))
        bounds.append((k + 1) * unit)
    gates.append(switch_all)
    names.append(jnp.ones_like(switch_all))
    bounds.append(used)
    gates = pad_to(jnp.stack(gates + names, axis=1), 1, 128)

    down = None
    for k in range(n_sh):
        down = place_columns(down_pieces[k], 1, down, my_sh ^ k, parts)
    up_all = both_cores(tie(up_core, gates, down))
    act_low, pre_grad, gate_terms = hidden_units(
        normed_two, up_all, gate_up, down, gates, tuple(bounds)
    )
    lane = lax.broadcasted_iota(jnp.int32, (1, 128), 1)
    gate_terms = sum(
        jnp.where(lane == (first_expert + k if k < per else experts), gate_terms[:, k : k + 1], 0.0)
        for k in range(per + 1)
    )
    half = total // 2
    peers = n_sh * n_tp // 2

    def grad_whole(units, which, values):
        whole = units_dot(units, which, used, values, parts)
        if parts == n_ctx:
            return whole
        whole = whole.reshape(used, n_sh, n_ctx, own)
        return whole.transpose(2, 0, 1, 3).reshape(n_ctx, used, -1)

    def sum_ctx_parts(whole):
        return lax.psum_scatter(whole, "ctx", scatter_dimension=0, tiled=True)

    def sum_core(left, right, urgent, between=None):
        sent = rows_dot(left, 1, right, None, urgent)
        arrived = swap(sent, "tp", 1)
        if between is not None:
            left = tie(left, between(sent))
        return rows_dot(left, 0, right, arrived, urgent)

    def by_shard(own):
        own = own.reshape(n_sh, n_tp // 2, part, own.shape[-1])
        return [pick(own, my_sh ^ k, 0) for k in range(n_sh)]

    gate_terms = gate_terms.reshape(2, half, gate_terms.shape[-1])
    gate_terms = (gate_terms[0] + swap(gate_terms[1], "tp", 1)).astype(bf16)
    down_whole = []

    def down_dot(after):
        down_whole.append(grad_whole(tie(act_low, after), 0, up_all))
        return down_whole[0]

    own_grad = sum_core(pre_grad, gate_up, True, down_dot)
    down_piece = sum_ctx_parts(down_whole[0])
    own_grad = by_shard(jnp.concatenate([own_grad, gate_terms], axis=1))
    own_mixed = sum_core(tie(act_low, *own_grad), down, False)
    own_grad = [tie(v, own_mixed) for v in others(own_grad, "shard")]
    mixed = [tie(v, *own_grad) for v in by_shard(own_mixed)]
    mixed = others(mixed, "shard")
    grad_kept, grad_sent = sum_shard(own_grad)
    gate_whole = grad_whole(tie(pre_grad, grad_sent), 0, normed_two)
    gate_piece = sum_ctx_parts(gate_whole)
    normed_grad = grad_kept + tie(swap_z(grad_sent), gate_whole)
    gate_terms = normed_grad[:, width:]
    normed_grad = from_parts(normed_grad[:, :width])

    def owned(piece):
        return [
            lax.dynamic_slice_in_dim(piece[0], (my_sh ^ k) * own, own, 1) for k in range(n_sh)
        ]

    def settle(pieces, *after):
        return unpack([tie(p, *after) for p in pieces], my_sh, mine_first)

    def turned(one, two):
        one = one.reshape(experts, hidden, own).transpose(0, 2, 1)
        return one, two.reshape(shared_hidden, own).T

    my_probs, my_switch = route(my_normed, routing)
    prob_grads = gate_terms[:, :experts]
    logit_grads = my_probs * (
        prob_grads - jnp.sum(my_probs * prob_grads, axis=-1, keepdims=True)
    )
    switch_pre_grad = gate_terms[:, experts] * my_switch * (1.0 - my_switch)
    route_grads = jnp.concatenate([logit_grads, switch_pre_grad[:, None]], axis=1)
    normed_float = my_normed.astype(f32)
    routing_grad = lax.dot_general(
        route_grads, normed_float, (((0,), (0,)), ((), ())), precision=highest
    )
    normed_grad = normed_grad + lax.dot_general(
        route_grads, routing.astype(f32), (((1,), (1,)), ((), ())), precision=highest
    )
    hidden_norm_grad, ffn_gain_grad = second_pull(normed_grad)
    hidden_grad = my_up + hidden_norm_grad

    def pieces_of(terms):
        return [pick(terms, my_sh ^ k, 0) for k in range(n_sh)]

    def sum_pieces(pieces, *after):
        return sum(tie(piece, *after).astype(f32) for piece in others(pieces, "shard"))

    def for_other(terms):
        return pick(terms, 1 - my_ctx, 0).astype(bf16)


    my_branch = hidden_grad.astype(bf16)
    up_whole = grad_whole(tie(pre_grad, my_branch), 1, normed_two)
    up_piece = sum_ctx_parts(up_whole)
    down_terms = others(owned(down_piece), "shard")
    mixed_kept, mixed_sent = sum_shard([tie(v, my_branch) for v in mixed])
    mixed_got = swap(mixed_sent, "tp", 2)
    branch_low = tie(gather_tp(my_branch), up_whole, mixed_got, *down_terms)
    out_weight_grad = dot_rows(head_rows, branch_low).astype(bf16)
    out_terms = [
        lax.dynamic_slice_in_dim(out_weight_grad, (my_sh ^ k) * n_ctx * own, n_ctx * own, 1)
        for k in range(n_sh)
    ]
    head_grad = dot_cols(branch_low, out_full).astype(bf16)
    head_grad = heads(head_grad)
    prob_grad = jnp.einsum("mhqd,mhkd->mhqk", head_grad, value_all, preferred_element_type=f32)
    value_grad = jnp.einsum("mhqk,mhqd->mhkd", probs_low, head_grad, preferred_element_type=f32)
    score_low = (
        probs * (prob_grad - jnp.sum(probs * prob_grad, axis=-1, keepdims=True))
    ).astype(bf16)
    query_grad = jnp.einsum("mhqk,mhkd->mhqd", score_low, key_all, preferred_element_type=f32)
    key_grad = jnp.einsum("mhqk,mhqd->mhkd", score_low, query_rows, preferred_element_type=f32)
    pair_grad = jnp.stack([key_grad, value_grad])
    pair_sent = pair_grad[..., rows:, :].astype(bf16)
    arrived = swap(pair_sent, "ctx", 1)
    down_parts = settle(down_terms, pair_sent)
    expert_down_grad = down_parts[0].reshape(experts, hidden, own)
    shared_down_grad = down_parts[1].reshape(shared_hidden, own)
    out_summed = sum_pieces(out_terms, pair_sent)
    gate_parts = settle(others(owned(gate_piece), "shard"), pair_sent)
    arrived = tie(arrived, *down_parts, out_summed, *gate_parts)
    key_grad, value_grad = pair_grad[..., :rows, :] + arrived.astype(f32)
    proj_grad = jnp.concatenate(
        [
            flat(rotate(query_grad * score_scale, cosine, -sine_table).astype(bf16)),
            flat(rotate(key_grad * score_scale, cosine, -sine_table).astype(bf16)),
            flat(value_grad.astype(bf16)),
        ],
        axis=1,
    )
    qkv_grad = dot_rows(normed_one, proj_grad).astype(bf16)
    qkv_terms = qkv_grad.reshape(n_sh, n_ctx * own, -1)
    in_square = n_sh == 4
    if in_square:
        my_x, my_y = my_sh % 2, my_sh // 2
        middle = qkv_terms.shape[2] // 2
        qkv_terms = qkv_terms.reshape(2, 2, n_ctx * own, -1)
        one_half, two_half = qkv_terms[..., :middle], qkv_terms[..., middle:]
        kept_terms = pick(one_half, my_x, 1), pick(two_half, my_y, 0)
        qkv_terms = [pick(one_half, 1 - my_x, 1), pick(two_half, 1 - my_y, 0)]
    else:
        qkv_terms = pieces_of(qkv_terms)
    one_terms = dot_cols(tie(proj_grad, *qkv_terms), qkv_full)
    count = n_sh * n_ctx
    bias_own = head_dim // count
    bias_grad = jnp.sum(proj_grad.astype(f32), axis=0)
    bias_grad = bias_grad.reshape(3 * local_heads, head_dim)
    wide = inputs.astype(f32)
    factor = lax.rsqrt(jnp.mean(wide * wide, axis=-1, keepdims=True) + epsilon)
    attn_gain_grad = jnp.sum(one_terms * (wide * factor), axis=0, keepdims=True)
    late = jnp.concatenate([routing_grad, ffn_gain_grad[None], attn_gain_grad], axis=0)
    late = jnp.concatenate(
        [
            late.reshape(-1, count, own).transpose(1, 0, 2).reshape(count, -1),
            bias_grad.reshape(-1, count, bias_own).transpose(1, 0, 2).reshape(count, -1),
        ],
        axis=1,
    )
    expert_gate_grad, shared_gate_grad = turned(*gate_parts)
    mixed_sum = mixed_kept + tie(mixed_got, one_terms).astype(f32)
    my_out = (hidden_res + from_parts(mixed_sum)).astype(bf16)
    out_summed = tie(out_summed, one_terms).reshape(-1, n_ctx, own).transpose(1, 0, 2)
    out_got = swap(for_other(out_summed), "ctx", 1)
    out_weight_grad = pick(out_summed, my_ctx, 0) + out_got.astype(f32)
    normed_one_grad = sum_tp(one_terms.reshape(n_tp, part, width))
    if in_square:
        one_half = kept_terms[0].astype(f32) + swap(qkv_terms[0], "shard", 1).astype(f32)
        two_half = kept_terms[1].astype(f32) + swap(qkv_terms[1], "shard", 2).astype(f32)
        kept_terms = pick(one_half, my_y, 0), pick(two_half, my_x, 0)
        qkv_terms = [
            pick(one_half, 1 - my_y, 0).astype(bf16),
            pick(two_half, 1 - my_x, 0).astype(bf16),
        ]
        qkv_terms = [swap(qkv_terms[0], "shard", 2), swap(qkv_terms[1], "shard", 1)]
    _, first_pull = jax.vjp(lambda v: rms_scale(v, first_gain), my_inputs)
    (input_norm_grad,) = first_pull(normed_one_grad)
    my_tokens_grad = tie((hidden_grad + input_norm_grad).astype(bf16), out_got, *(qkv_terms if in_square else []))
    tokens_grad = gather_tp(my_tokens_grad).astype(f32)
    late = jnp.broadcast_to(tie(late, my_tokens_grad)[:, None], (count, n_tp, late.shape[1]))
    late_rows = lax.all_to_all(
        late.reshape(count * n_tp, -1), ("shard", "ctx", "tp"), 0, 0, tiled=True
    ).reshape(late.shape)
    at = (experts + 3) * own
    late_sum = jnp.sum(late_rows[:, :, :at], axis=(0, 1))
    bias_grad = jnp.sum(pick(late_rows[:, :, at:], my_tp, 1), axis=0)
    bias_grad = bias_grad.reshape(3, local_heads, bias_own)
    late = late_sum.reshape(experts + 3, own)
    if in_square:
        qkv_summed = jnp.concatenate(
            [
                kept + tie(got, my_tokens_grad).astype(f32)
                for kept, got in zip(kept_terms, qkv_terms)
            ],
            axis=1,
        )
    else:
        qkv_summed = sum_pieces(qkv_terms, my_tokens_grad)
    qkv_summed = qkv_summed.reshape(n_ctx, own, -1)
    qkv_sent = for_other(qkv_summed)
    up_terms = others(owned(tie(up_piece, qkv_sent)), "shard")
    qkv_got = swap(qkv_sent, "ctx", 1)
    qkv_grad = pick(qkv_summed, my_ctx, 0) + qkv_got.astype(f32)
    qkv_grad = qkv_grad.reshape(own, 3, heads_width).transpose(1, 0, 2)

    layer_out = gather_tp(tie(my_out, qkv_sent))
    expert_up_grad, shared_up_grad = turned(*settle(up_terms, qkv_got))
    shape = (micro, 1, rows, width)
    return (
        layer_out.reshape(shape),
        tokens_grad.reshape(shape),
        late[experts + 2],
        qkv_grad,
        bias_grad,
        out_weight_grad,
        late[experts + 1],
        late[:experts].T,
        expert_gate_grad,
        expert_up_grad,
        expert_down_grad,
        shared_gate_grad,
        shared_up_grad,
        shared_down_grad,
        late[experts],
    )


def solution(mesh):
    in_specs = (
        P(None, "shard", "ctx", None),
        P(None, "shard", "ctx", None),
        P(None, "shard", "ctx", None),
        P(None, "shard"),
        P("shard"),
        P(None, "shard", "tp"),
        P(None, "tp", None),
        P("tp", "shard"),
        P("shard"),
        P("shard", None),
        P(None, "shard", "tp"),
        P(None, "shard", "tp"),
        P(None, "tp", "shard"),
        P("shard", "tp"),
        P("shard", "tp"),
        P("tp", "shard"),
        P("shard"),
    )
    out_specs = (
        P(None, "shard", "ctx", None),
        P(None, "shard", "ctx", None),
        P(("shard", "ctx")),
        P(None, ("shard", "ctx"), "tp"),
        P(None, "tp", ("shard", "ctx")),
        P("tp", ("shard", "ctx")),
        P(("shard", "ctx")),
        P(("shard", "ctx"), None),
        P(None, ("shard", "ctx"), "tp"),
        P(None, ("shard", "ctx"), "tp"),
        P(None, "tp", ("shard", "ctx")),
        P(("shard", "ctx"), "tp"),
        P(("shard", "ctx"), "tp"),
        P("tp", ("shard", "ctx")),
        P(("shard", "ctx")),
    )
    return jax.shard_map(body, mesh=mesh, in_specs=in_specs, out_specs=out_specs, check_vma=False)
```
